32 devices in a mesh: dp: 4 (over x, core), space: 8 (over z, y).
Axes of the slice: x: 2, y: 2, z: 4, core: 2. Of those that a mesh axis runs over, the one named last changes fastest.
Arguments:
- volume: bfloat16 [4, 4, 64, 8, 256], P('dp', None, 'space'), may hold values from -6 to 6
- first_filters: bfloat16 [16, 4, 3, 3, 3], replicated, may hold values from -0.625 to 0.625
- first_biases: float32 [16], replicated, may hold values from -0.5 to 0.5
- second_filters: bfloat16 [32, 16, 3, 3, 3], replicated, may hold values from -0.3125 to 0.3125
- second_biases: float32 [32], replicated, may hold values from -0.5 to 0.5
- cotangent: bfloat16 [4, 32, 32, 4, 128], P('dp', None, 'space'), may hold values from -12 to 12
Outputs:
- activations: bfloat16 [4, 32, 32, 4, 128], P('dp', None, 'space')
- pooled_grad: bfloat16 [4, 16, 32, 4, 128], P('dp', None, 'space')
- gradient_one: float32 [16, 4, 3, 3, 3], replicated
- shift_one: float32 [16], replicated
- gradient_two: float32 [32, 16, 3, 3, 3], replicated
- shift_two: float32 [32], replicated
The draws below stay inside these ranges and needn't reach their ends.
All inputs are finite; a program needn't handle non-finite values.
Results may differ from the reference program's by a relative error of at most 0.015.
The reference program's roundings to bfloat16 on the way (of `pooled_one`, `delta_two` and `delta_one`) count: a program that leaves them out, or rounds other values in their place, can miss the bound.
Values may be sent and summed in bfloat16 or wider, within the bound.
A program may use at most 128 MiB of HBM per device.

```python
import math
import jax
import jax.numpy as jnp
from jax import lax

C_IN = 4
C1 = 16
C2 = 32
HEIGHT = 8
WIDTH = 256
SAMPLES = 4
DEPTH = 64


def draw_cotangent(key, part):
    extent = (SAMPLES, C2, DEPTH // 2, HEIGHT // 2, WIDTH // 2)
    first_key = jax.random.fold_in(key, 0)
    sample_rise = jnp.arange(SAMPLES, dtype=jnp.float32) / max(SAMPLES - 1, 1)
    depth_rise = jnp.arange(DEPTH // 2, dtype=jnp.float32) / max(DEPTH // 2 - 1, 1)
    factor = jnp.exp(math.log(3.0) * (sample_rise[:, None, None, None, None] + depth_rise[None, None, :, None, None] - 1.0))
    values = jax.random.truncated_normal(first_key, -4.0, 4.0, extent, jnp.float32)
    return (values * factor).astype(jnp.bfloat16)


def level_of(rng, dims, cuts, smallest, largest):
    loudness = 1.0
    for dim, parts in cuts:
        heights = jax.random.uniform(jax.random.fold_in(jax.random.fold_in(rng, 6), dim), (parts,), jnp.float32, smallest / len(cuts), largest / len(cuts))
        loudness = loudness * jnp.repeat(jnp.exp(heights), dims[dim] // parts).reshape((-1,) + (1,) * (len(dims) - 1 - dim))
    return loudness


def centred(stream_key, shape, width, limit, cuts=(), kind=jnp.bfloat16):
    entries = width * jax.random.normal(stream_key, shape, jnp.float32)
    if cuts:
        entries = entries * level_of(stream_key, shape, cuts, -0.22, 0.18)
    return jnp.clip(entries, -limit, limit).astype(kind)


def setup_inputs(seed: int = 0) -> dict:
    seeds = jax.random.split(jax.random.key(seed), 7)
    return {
        "volume": centred(seeds[0], (SAMPLES, C_IN, DEPTH, HEIGHT, WIDTH), 1.0, 6.0, ((0, 4), (2, 8))),
        "first_filters": centred(seeds[1], (C1, C_IN, 3, 3, 3), (C_IN * 27) ** -0.5, 0.625),
        "first_biases": jnp.clip(jax.random.uniform(seeds[2], (C1,), jnp.float32, -0.5, 0.5), -0.5, 0.5),
        "second_filters": centred(seeds[3], (C2, C1, 3, 3, 3), (C1 * 27) ** -0.5, 0.3125),
        "second_biases": jnp.clip(jax.random.uniform(seeds[4], (C2,), jnp.float32, -0.5, 0.5), -0.5, 0.5),
        "cotangent": draw_cotangent(jax.random.fold_in(seeds[6], 71), 0),
    }


def convolve(padded, kernel):
    return lax.conv_general_dilated(padded[None].astype(jnp.float32), kernel.astype(jnp.float32), (1, 1, 1), 'VALID', dimension_numbers=('NCDHW', 'OIDHW', 'NCDHW'), precision=lax.Precision.HIGHEST)[0]

def pad_all(values):
    return jnp.pad(values, ((0, 0), (1, 1), (1, 1), (1, 1)))

def leaky_rectify(values):
    return jnp.where(values > 0, values, 0.3 * values)

def rectify_slope(values):
    return jnp.where(values > 0, 1.0, 0.3)

def mean_pool(values):
    extent = values.shape
    blocks = values.reshape(extent[0], extent[1] // 2, 2, extent[2] // 2, 2, extent[3] // 2, 2)
    return lax.optimization_barrier(jnp.sum(blocks, axis=(2, 4, 6))) * 0.125

def spread_up(values):
    extent = values.shape
    grown = jnp.broadcast_to(values[:, :, None, :, None, :, None], (extent[0], extent[1], 2, extent[2], 2, extent[3], 2))
    return grown.reshape(extent[0], 2 * extent[1], 2 * extent[2], 2 * extent[3])

def kernel_grad(padded, errors):
    outs_n = errors.shape[0]
    ins_n = padded.shape[0]
    depth_n, high_n, wide_n = (errors.shape[1], errors.shape[2], errors.shape[3])
    flat_errors = errors.reshape(outs_n, -1).astype(jnp.float32)
    tap_terms = []
    for depth_tap in range(3):
        for height_tap in range(3):
            for width_tap in range(3):
                window = padded[:, depth_tap:depth_tap + depth_n, height_tap:height_tap + high_n, width_tap:width_tap + wide_n]
                window = window.reshape(ins_n, -1).astype(jnp.float32)
                tap_terms.append(jnp.dot(flat_errors, window.T, precision=lax.Precision.HIGHEST))
    stacked = jnp.stack(tap_terms, 0).reshape(3, 3, 3, outs_n, ins_n)
    return stacked.transpose(3, 4, 0, 1, 2)

def reference(volume, first_filters, first_biases, second_filters, second_biases, cotangent):
    flipped = jnp.flip(second_filters, (2, 3, 4)).transpose(1, 0, 2, 3, 4)

    def one_sample(paired):
        sample, target = paired
        first_in = pad_all(sample)
        linear_one = convolve(first_in, first_filters) + first_biases[:, None, None, None]
        pooled_one = mean_pool(leaky_rectify(linear_one)).astype(jnp.bfloat16)
        second_in = pad_all(pooled_one)
        linear_two = convolve(second_in, second_filters) + second_biases[:, None, None, None]
        activations = leaky_rectify(linear_two).astype(jnp.bfloat16)
        delta_two = (target.astype(jnp.float32) * rectify_slope(linear_two)).astype(jnp.bfloat16)
        grad_two = kernel_grad(second_in, delta_two)
        bias_two = lax.optimization_barrier(jnp.sum(delta_two.astype(jnp.float32), axis=(1, 2, 3)))
        pooled_grad = convolve(pad_all(delta_two), flipped).astype(jnp.bfloat16)
        stored_grad = lax.optimization_barrier(pooled_grad)
        delta_one = (spread_up(stored_grad.astype(jnp.float32)) * 0.125 * rectify_slope(linear_one)).astype(jnp.bfloat16)
        grad_one = kernel_grad(first_in, delta_one)
        bias_one = lax.optimization_barrier(jnp.sum(delta_one.astype(jnp.float32), axis=(1, 2, 3)))
        return (activations, pooled_grad, grad_one, bias_one, grad_two, bias_two)
    results = lax.map(one_sample, (volume, cotangent))
    count_one = SAMPLES * DEPTH * HEIGHT * WIDTH
    scale_one = 1.0 / math.sqrt(count_one)
    scale_two = 1.0 / math.sqrt(count_one / 8)
    return (results[0], results[1], lax.optimization_barrier(jnp.sum(results[2], 0)) * scale_one, lax.optimization_barrier(jnp.sum(results[3], 0)) * scale_one, lax.optimization_barrier(jnp.sum(results[4], 0)) * scale_two, lax.optimization_barrier(jnp.sum(results[5], 0)) * scale_two)
```

```python
import functools
import math

import jax
import jax.numpy as jnp
import numpy as np
from jax import lax
from jax.experimental import pallas as pl
from jax.experimental.pallas import tpu as pltpu
from jax.sharding import PartitionSpec as P

BF = jnp.bfloat16
F32 = jnp.float32
MESH = pl.DeviceIdType.MESH
LANES = 128
RIM = 48
TILES = 16


def tap_choice():
    table = np.zeros((2, 2, 3, 4, 4, 4, 128), np.float32)
    for dd in range(2):
        for wpar in range(2):
            for kh in range(3):
                for s in range(4):
                    for dz in range(4):
                        kd, kw = dz - dd, s - wpar
                        if 0 <= kd < 3 and 0 <= kw < 3:
                            for i in range(4):
                                table[dd, wpar, kh, s, i, dz, ((kd * 3 + kh) * 3 + kw) * 4 + i] = 1
    return table.reshape(4 * 192, 128)


def iota(shape, dim):
    return lax.broadcasted_iota(jnp.int32, shape, dim)


def dot(a, b):
    return jnp.dot(a, b, preferred_element_type=F32)


def dot_nt(a, b):
    return lax.dot_general(a, b, (((1,), (1,)), ((), ())), preferred_element_type=F32)


def column(row, count):
    return jnp.sum(
        jnp.where(iota((count, count), 0) == iota((count, count), 1), row, 0.0),
        axis=1,
        keepdims=True,
    )


def fold(values, steps):
    for step in steps:
        values = values + pltpu.roll(values, step, axis=values.ndim - 1)
    return values


def kernel(
    dp_n, space_n, scale_one, scale_two,
    vol, cot, f1, f2, b1, b2, choice,
    act_out, pg_out, g1_out, s1_out, g2_out, s2_out,
    raw, cots, cotf, shifted, pooled, slopes, errors_two, errors_one, pgf, w1, w2, w2t,
    stack, terms, landed, across, total,
    halo_send, halo_recv, rs_send, rs_recv, dp_send, dp_recv, ag_send, ag_recv,
):
    me = lax.axis_index("space")
    mine = lax.axis_index("dp")
    first = me == 0
    last = me == space_n - 1

    barrier = pltpu.get_barrier_semaphore()
    for k in range(1, space_n):
        pl.semaphore_signal(
            barrier, inc=1, device_id={"space": lax.rem(me + k, space_n)}, device_id_type=MESH
        )
    for k in range(1, dp_n):
        pl.semaphore_signal(
            barrier, inc=1, device_id={"dp": lax.rem(mine + k, dp_n)}, device_id_type=MESH
        )

    cotf[...] = cot[...].reshape(512, LANES).astype(F32)
    for d in range(4):
        for hq in range(4):
            cots[pl.ds((1 + d) * 128 + hq * 32, 32), :] = cotf[
                pl.ds(d * 4 + hq, 32, stride=16), :
            ].astype(BF)
    raw[:, RIM : RIM + 64, :] = vol[...]

    @pl.when(first)
    def _():
        raw[:, 0:RIM, :] = jnp.zeros((4, RIM, 256), BF)
        cots[0:128, :] = jnp.zeros((128, LANES), BF)

    @pl.when(last)
    def _():
        raw[:, RIM + 64 :, :] = jnp.zeros((4, RIM, 256), BF)
        cots[640:768, :] = jnp.zeros((128, LANES), BF)

    pl.semaphore_wait(barrier, space_n - 1 + dp_n - 1)

    right = lax.rem(me + 1, space_n)
    left = lax.rem(me + space_n - 1, space_n)

    def halo(which):
        src, dst, to = (
            (raw.at[:, 64 : 64 + RIM], raw.at[:, 0:RIM], right),
            (raw.at[:, RIM : 2 * RIM], raw.at[:, RIM + 64 : 2 * RIM + 64], left),
            (cots.at[512:640], cots.at[0:128], right),
            (cots.at[128:256], cots.at[640:768], left),
        )[which]
        return pltpu.make_async_remote_copy(
            src_ref=src,
            dst_ref=dst,
            send_sem=halo_send.at[which],
            recv_sem=halo_recv.at[which],
            device_id={"space": to},
            device_id_type=MESH,
        )

    @pl.when(jnp.logical_not(last))
    def _():
        halo(0).start()
        halo(2).start()

    @pl.when(jnp.logical_not(first))
    def _():
        halo(1).start()
        halo(3).start()

    lane = iota((64, 512), 1)
    group = iota((64, 512), 0)
    spread = (
        (lane % 16 == group % 16) & (lane // 256 == group // 32) & ((lane // 64) % 2 == (group // 16) % 2)
    ).astype(F32).astype(BF)
    picked = dot(choice[...], f1[...]).astype(BF)
    rows = jnp.concatenate([picked[g * 192 : (g + 1) * 192] for g in range(4)], axis=1)
    rows = dot(rows, spread)
    lane8 = iota((8, 512), 1)
    reach = iota((8, 512), 0) - (2 * ((lane8 // 16) % 4) + (lane8 // 128) % 2) + 1
    near = [reach == kh for kh in range(3)]
    matrix = jnp.zeros((64, 8, 512), F32)
    for kh in range(3):
        piece = rows[kh * 64 : (kh + 1) * 64].reshape(64, 1, 512)
        matrix = jnp.where(near[kh][None], piece, matrix)
    w1[...] = matrix.reshape(512, 512).T.astype(BF)

    tile4 = (iota((32, 128), 0) == iota((32, 128), 1) % 32).astype(F32).astype(BF)
    wide = dot(f2[...], tile4)
    group4 = iota((16, 128), 1) // 32
    parts = []
    for kd in range(3):
        for kw in range(3):
            for hq in range(4):
                block = jnp.zeros((16, 128), F32)
                for kh in range(3):
                    if 0 <= hq - kh + 1 < 4:
                        tap = (kd * 3 + kh) * 3 + kw
                        block = jnp.where(group4 == hq - kh + 1, wide[tap * 16 : tap * 16 + 16], block)
                parts.append(block)
    joined = jnp.concatenate(parts, axis=0)
    w2t[...] = joined.astype(BF)
    w2[...] = joined.T.astype(BF)

    bias_one = column(b1[...], 16)
    bias_two = column(b2[...], 32)
    take = iota((256, 512), 1)
    sample = (iota((256, 512), 0) == 2 * (take % 128) - 1 + take // 128).astype(F32).astype(BF)

    @pl.when(jnp.logical_not(last))
    def _():
        halo(1).wait_recv()

    @pl.when(jnp.logical_not(first))
    def _():
        halo(0).wait_recv()

    columns = dot(raw[...].reshape(4 * 160, 256), sample).reshape(4, 160, 512)[:, 8:152]
    for s in range(4):
        shifted[s * 4 : s * 4 + 4] = columns[:, :, s * 128 : (s + 1) * 128].astype(BF)

    lane64 = iota((64, 128), 1)

    def window(p):
        return shifted[:, pl.ds(pl.multiple_of(p * 16, 16), 32), :].reshape(512, LANES)

    def layer_one(p, carry):
        linear = dot(w1[...], window(p)).reshape(32, 16, LANES) + bias_one[None]
        linear = linear.reshape(8, 64, LANES)
        slope = jnp.where(linear > 0, 1.0, 0.3)
        slopes[p] = slope
        mean = jnp.sum(linear * slope, axis=0) * 0.125
        outside = (first & (p < 2)) | (last & (p > 5))
        mean = jnp.where(outside, 0.0, mean)
        base = pl.multiple_of(p * 192, 16)
        pooled[pl.ds(base, 64), :] = jnp.where(lane64 == 0, 0.0, pltpu.roll(mean, 1, axis=1)).astype(BF)
        pooled[pl.ds(base + 64, 64), :] = mean.astype(BF)
        pooled[pl.ds(base + 128, 64), :] = jnp.where(
            lane64 == 127, 0.0, pltpu.roll(mean, 127, axis=1)
        ).astype(BF)
        return carry

    lax.fori_loop(0, 8, layer_one, 0)

    @pl.when(jnp.logical_not(last))
    def _():
        halo(3).wait_recv()

    @pl.when(jnp.logical_not(first))
    def _():
        halo(2).wait_recv()

    for j in range(6):
        linear = dot(w2[...], pooled[j * 192 : j * 192 + 576, :]).reshape(4, 32, LANES)
        linear = (linear + bias_two[None]).reshape(128, LANES)
        slope = jnp.where(linear > 0, 1.0, 0.3)
        errors_two[j * 128 : (j + 1) * 128, :] = (
            cots[j * 128 : (j + 1) * 128, :].astype(F32) * slope
        ).astype(BF)
        if 1 <= j <= 4:
            out = linear * slope
            for hq in range(4):
                cotf[pl.ds((j - 1) * 4 + hq, 32, stride=16), :] = out[hq * 32 : (hq + 1) * 32]
    act_out[...] = cotf[...].astype(BF).reshape(32, 16, LANES)

    own = jnp.concatenate(
        [errors_two[j * 128 : (j + 1) * 128, :] for j in range(1, 5)], axis=1
    )
    near_in = jnp.concatenate(
        [pooled[j * 192 : j * 192 + 576, :] for j in range(1, 5)], axis=1
    )
    near_in = jnp.concatenate([near_in, jnp.ones((16, 512), BF)], axis=0)
    outer = dot_nt(near_in, own)
    taps = []
    for kd in range(3):
        for kh in range(3):
            for kw in range(3):
                block = jnp.zeros((16, 128), F32)
                for hq in range(4):
                    if 0 <= hq - kh + 1 < 4:
                        at = ((kd * 3 + kw) * 4 + hq) * 16
                        block = jnp.where(group4 == hq - kh + 1, outer[at : at + 16], block)
                taps.append(fold(block, (64, 32)))
    taps.append(fold(outer[576:592], (64, 32)))
    for q in range(7):
        block = taps[4 * q]
        for slot in range(1, 4):
            block = jnp.where(group4 == slot, taps[4 * q + slot], block)
        terms[2 * q] = block[0:8]
        terms[2 * q + 1] = block[8:16]

    back = jnp.concatenate([w2t[kd * 192 : (kd + 1) * 192, :] for kd in (2, 1, 0)], axis=1)
    for q in range(4):
        three = dot(back, errors_two[q * 128 : q * 128 + 384, :])
        grad = three[64:128]
        grad = grad + jnp.where(lane64 == 127, 0.0, pltpu.roll(three[0:64], 127, axis=1))
        grad = grad + jnp.where(lane64 == 0, 0.0, pltpu.roll(three[128:192], 1, axis=1))
        grad = grad.astype(BF).astype(F32)
        for hq in range(4):
            pgf[pl.ds(q * 4 + hq, 16, stride=16), :] = grad[hq * 16 : (hq + 1) * 16]
        errors_one[:, q * 128 : (q + 1) * 128] = (
            ((grad * 0.125)[None] * slopes[q + 2]).astype(BF).reshape(512, LANES)
        )
    pg_out[...] = pgf[...].astype(BF).reshape(16, 16, LANES)

    near_in = jnp.concatenate([window(p) for p in range(2, 6)], axis=1)
    near_in = jnp.concatenate([near_in, jnp.ones((16, 512), BF)], axis=0)
    outer = dot_nt(near_in, errors_one[...])
    body = outer[0:512].reshape(4, 4, 4, 8, 512)
    low = iota((4, 3, 8, 128), 3) < 64
    for kh in range(3):
        summed = jnp.zeros((4, 4, 3, 8, 128), F32)
        for part in range(4):
            dd = part // 2
            cut = body[:, :, dd : dd + 3, :, part * 128 : (part + 1) * 128]
            mask = near[kh][:, part * 128 : (part + 1) * 128]
            summed = summed + jnp.where(mask[None, None, None], cut, 0.0)
        for kw in range(3):
            both = jnp.where(low, summed[kw], summed[kw + 1])
            for kd in range(3):
                tap = (kd * 3 + kh) * 3 + kw
                stack[tap * 32 : tap * 32 + 32, :] = both[:, kd].reshape(32, LANES)
    ones = outer[512:520]
    ones = ones[:, 0:128] + ones[:, 128:256] + ones[:, 256:384] + ones[:, 384:512]
    stack[864:872, :] = jnp.where(iota((8, 128), 0) == 0, ones, 0.0)
    stack[872:896, :] = jnp.zeros((24, 128), F32)
    gather = (iota((112, 896), 0) == iota((112, 896), 1) // 8).astype(F32).astype(BF)
    whole = stack[...]
    high = whole.astype(BF)
    rest = (whole - high.astype(F32)).astype(BF)
    reduced = fold(dot(gather, high) + dot(gather, rest), (64, 32, 16))
    group8 = iota((8, 128), 1) // 16
    for half in range(2):
        block = jnp.zeros((8, 128), F32)
        for slot in range(8):
            v = half * 8 + slot
            if v < 14:
                block = jnp.where(group8 == slot, reduced[v * 8 : v * 8 + 8], block)
        terms[14 + half] = block

    share = TILES // space_n

    def scatter(k):
        to = lax.rem(me + k, space_n)
        return pltpu.make_async_remote_copy(
            src_ref=terms.at[pl.ds(to * share, share)],
            dst_ref=landed.at[k - 1],
            send_sem=rs_send.at[k - 1],
            recv_sem=rs_recv.at[k - 1],
            device_id={"space": to},
            device_id_type=MESH,
        )

    for k in range(1, space_n):
        scatter(k).start()
    sums = terms[pl.ds(me * share, share)]
    for k in range(1, space_n):
        scatter(k).wait_recv()
        sums = sums + landed[k - 1]
    across[mine] = sums

    def exchange(k):
        to = lax.rem(mine + k, dp_n)
        return pltpu.make_async_remote_copy(
            src_ref=across.at[mine],
            dst_ref=across.at[mine],
            send_sem=dp_send.at[k - 1],
            recv_sem=dp_recv.at[k - 1],
            device_id={"dp": to},
            device_id_type=MESH,
        )

    def arrival(k):
        source = lax.rem(mine + dp_n - k, dp_n)
        return pltpu.make_async_remote_copy(
            src_ref=across.at[source],
            dst_ref=across.at[source],
            send_sem=dp_send.at[k - 1],
            recv_sem=dp_recv.at[k - 1],
            device_id={"dp": source},
            device_id_type=MESH,
        )

    for k in range(1, dp_n):
        exchange(k).start()
    for k in range(1, dp_n):
        arrival(k).wait_recv()
    sums = across[0]
    for k in range(1, dp_n):
        sums = sums + across[k]
    total[pl.ds(me * share, share)] = sums

    def spread_out(k, source):
        return pltpu.make_async_remote_copy(
            src_ref=total.at[pl.ds(source * share, share)],
            dst_ref=total.at[pl.ds(source * share, share)],
            send_sem=ag_send.at[k - 1],
            recv_sem=ag_recv.at[k - 1],
            device_id={"space": lax.rem(me + k, space_n)},
            device_id_type=MESH,
        )

    for k in range(1, space_n):
        spread_out(k, me).start()
    for k in range(1, space_n):
        spread_out(k, lax.rem(me + space_n - k, space_n)).wait_recv()

    for q in range(7):
        block = jnp.concatenate([total[2 * q], total[2 * q + 1]], axis=0) * scale_two
        for slot in range(4):
            tap = 4 * q + slot
            turned = block if slot == 0 else pltpu.roll(block, 128 - 32 * slot, axis=1)
            if tap < 27:
                g2_out[tap * 16 : tap * 16 + 16, :] = turned[:, 0:32]
            else:
                s2_out[...] = turned[0:1, 0:32]
    for v in range(14):
        block = total[14 + v // 8] * scale_one
        slot = v % 8
        turned = block if slot == 0 else pltpu.roll(block, 128 - 16 * slot, axis=1)
        if v < 13:
            g1_out[v * 8 : v * 8 + 8, :] = turned[:, 0:16]
        else:
            g1_out[104:108, :] = turned[0:4, 0:16]
            s1_out[...] = turned[4:5, 0:16]

    for k in range(1, space_n):
        scatter(k).wait_send()
        spread_out(k, me).wait_send()
    for k in range(1, dp_n):
        exchange(k).wait_send()

    @pl.when(jnp.logical_not(last))
    def _():
        halo(0).wait_send()
        halo(2).wait_send()

    @pl.when(jnp.logical_not(first))
    def _():
        halo(1).wait_send()
        halo(3).wait_send()


def shards(dp_n, space_n, volume, first_filters, first_biases, second_filters, second_biases, cotangent):
    _, c_in, planes, high, wide = volume.shape
    c1, c2 = first_filters.shape[0], second_filters.shape[0]
    assert (c_in, planes, high, wide, c1, c2) == (4, 8, 8, 256, 16, 32)
    assert TILES % space_n == 0
    count_one = dp_n * space_n * planes * high * wide
    scale_one = 1.0 / math.sqrt(count_one)
    scale_two = 1.0 / math.sqrt(count_one / 8)
    share = TILES // space_n
    f1 = first_filters.transpose(2, 3, 4, 1, 0).reshape(108, 16)
    f1 = jnp.pad(f1, ((0, 20), (0, 0)))
    f2 = second_filters.transpose(2, 3, 4, 1, 0).reshape(432, 32)
    vmem = pl.BlockSpec(memory_space=pltpu.VMEM)
    dma = pltpu.SemaphoreType.DMA
    act, pg, g1, s1, g2, s2 = pl.pallas_call(
        functools.partial(kernel, dp_n, space_n, scale_one, scale_two),
        out_shape=(
            jax.ShapeDtypeStruct((32, 16, 128), BF),
            jax.ShapeDtypeStruct((16, 16, 128), BF),
            jax.ShapeDtypeStruct((108, 16), F32),
            jax.ShapeDtypeStruct((1, 16), F32),
            jax.ShapeDtypeStruct((432, 32), F32),
            jax.ShapeDtypeStruct((1, 32), F32),
        ),
        in_specs=[vmem] * 7,
        out_specs=(vmem,) * 6,
        scratch_shapes=[
            pltpu.VMEM((4, 2 * RIM + 64, 256), BF),
            pltpu.VMEM((768, 128), BF),
            pltpu.VMEM((512, 128), F32),
            pltpu.VMEM((16, 144, 128), BF),
            pltpu.VMEM((8 * 192, 128), BF),
            pltpu.VMEM((8, 8, 64, 128), F32),
            pltpu.VMEM((768, 128), BF),
            pltpu.VMEM((512, 512), BF),
            pltpu.VMEM((256, 128), F32),
            pltpu.VMEM((512, 512), BF),
            pltpu.VMEM((128, 576), BF),
            pltpu.VMEM((576, 128), BF),
            pltpu.VMEM((896, 128), F32),
            pltpu.VMEM((TILES, 8, 128), F32),
            pltpu.VMEM((space_n - 1, share, 8, 128), F32),
            pltpu.VMEM((dp_n, share, 8, 128), F32),
            pltpu.VMEM((TILES, 8, 128), F32),
            dma((4,)),
            dma((4,)),
            dma((space_n - 1,)),
            dma((space_n - 1,)),
            dma((dp_n - 1,)),
            dma((dp_n - 1,)),
            dma((space_n - 1,)),
            dma((space_n - 1,)),
        ],
        compiler_params=pltpu.CompilerParams(
            collective_id=0, has_side_effects=True, vmem_limit_bytes=40 * 1024 * 1024
        ),
    )(
        volume.reshape(4, 64, 256),
        cotangent.reshape(32, 16, 128),
        f1,
        f2,
        first_biases.reshape(1, 16),
        second_biases.reshape(1, 32),
        jnp.asarray(tap_choice(), BF),
    )
    return (
        act.reshape(1, 32, 4, 4, 128),
        pg.reshape(1, 16, 4, 4, 128),
        g1.reshape(3, 3, 3, 4, 16).transpose(4, 3, 0, 1, 2),
        s1.reshape(16),
        g2.reshape(3, 3, 3, 16, 32).transpose(4, 3, 0, 1, 2),
        s2.reshape(32),
    )


def solution(mesh):
    placed = (
        P("dp", None, "space", None, None),
        P(),
        P(),
        P(),
        P(),
        P("dp", None, "space", None, None),
    )
    return jax.shard_map(
        functools.partial(shards, mesh.shape["dp"], mesh.shape["space"]),
        mesh=mesh,
        in_specs=placed,
        out_specs=(
            P("dp", None, "space", None, None),
            P("dp", None, "space", None, None),
            P(),
            P(),
            P(),
            P(),
        ),
        check_vma=False,
    )
```

```python
import functools
import math

import jax
import jax.numpy as jnp
import numpy as np
from jax import lax
from jax.experimental import pallas as pl
from jax.experimental.pallas import tpu as pltpu
from jax.sharding import PartitionSpec as P

BF = jnp.bfloat16
F32 = jnp.float32
MESH = pl.DeviceIdType.MESH
LANES = 128
RIM = 48
VMEM_LIMIT = 60 * 1024 * 1024
TILES = 16


def tap_choice():
    table = np.zeros((2, 2, 3, 4, 4, 4, 128), np.float32)
    for dd in range(2):
        for wpar in range(2):
            for kh in range(3):
                for s in range(4):
                    for dz in range(4):
                        kd, kw = dz - dd, s - wpar
                        if 0 <= kd < 3 and 0 <= kw < 3:
                            for i in range(4):
                                table[dd, wpar, kh, s, i, dz, ((kd * 3 + kh) * 3 + kw) * 4 + i] = 1
    return table.reshape(4 * 192, 128)


def iota(shape, dim):
    return lax.broadcasted_iota(jnp.int32, shape, dim)


def dot(a, b):
    return jnp.dot(a, b, preferred_element_type=F32)


def dot_nt(a, b):
    return lax.dot_general(a, b, (((1,), (1,)), ((), ())), preferred_element_type=F32)


def column(row, count):
    return jnp.sum(
        jnp.where(iota((count, count), 0) == iota((count, count), 1), row, 0.0),
        axis=1,
        keepdims=True,
    )


def fold(values, steps):
    for step in steps:
        values = values + pltpu.roll(values, step, axis=values.ndim - 1)
    return values


def kernel(
    dp_n, space_n,
    vol, cot, f1, f2, b1, b2, choice,
    act_out, pg_out, sums_out,
    raw, cotb, f1b, f1f, f2b, b1b, b2b, chosen,
    cots, cotf, shifted, pooled, slopes, errors_two, errors_one, pgf, w1, w2, w2t,
    stack, terms, landed, across, total, late, late_space, late_dp,
    act_here, pg_here, sums_here, out_sem, in_sem, halo_send, halo_recv, rs_send, rs_recv, dp_send, dp_recv, ag_send, ag_recv,
    ls_send, ls_recv, ld_send, ld_recv,
):
    me = lax.axis_index("space")
    mine = lax.axis_index("dp")
    first = me == 0
    last = me == space_n - 1

    barrier = pltpu.get_barrier_semaphore()
    for k in range(1, space_n):
        pl.semaphore_signal(
            barrier, inc=1, device_id={"space": lax.rem(me + k, space_n)}, device_id_type=MESH
        )
    for k in range(1, dp_n):
        pl.semaphore_signal(
            barrier, inc=1, device_id={"dp": lax.rem(mine + k, dp_n)}, device_id_type=MESH
        )
    loads = [
        pltpu.make_async_copy(src, dst, in_sem.at[n])
        for n, (src, dst) in enumerate(
            (
                (cot, cotb),
                (f1, f1b),
                (choice, chosen),
                (f2, f2b),
                (b1, b1b),
                (b2, b2b),
                (vol, raw.at[:, RIM : RIM + 64]),
            )
        )
    ]
    for load in loads:
        load.start()

    @pl.when(first)
    def _():
        raw[:, 0:RIM, :] = jnp.zeros((4, RIM, 256), BF)
        cots[0:128, :] = jnp.zeros((128, LANES), BF)

    @pl.when(last)
    def _():
        raw[:, RIM + 64 :, :] = jnp.zeros((4, RIM, 256), BF)
        cots[640:768, :] = jnp.zeros((128, LANES), BF)

    right = lax.rem(me + 1, space_n)
    left = lax.rem(me + space_n - 1, space_n)

    def halo(which):
        src, dst, to = (
            (vol.at[:, 16:64], raw.at[:, 0:RIM], right),
            (vol.at[:, 0:RIM], raw.at[:, RIM + 64 : 2 * RIM + 64], left),
            (cots.at[512:640], cots.at[0:128], right),
            (cots.at[128:256], cots.at[640:768], left),
        )[which]
        return pltpu.make_async_remote_copy(
            src_ref=src,
            dst_ref=dst,
            send_sem=halo_send.at[which],
            recv_sem=halo_recv.at[which],
            device_id={"space": to},
            device_id_type=MESH,
        )

    pl.semaphore_wait(barrier, space_n - 1 + dp_n - 1)

    @pl.when(jnp.logical_not(last))
    def _():
        halo(0).start()

    @pl.when(jnp.logical_not(first))
    def _():
        halo(1).start()

    loads[0].wait()
    cotf[...] = cotb[...].reshape(512, LANES).astype(F32)
    for d in range(4):
        for hq in range(4):
            cots[pl.ds((1 + d) * 128 + hq * 32, 32), :] = cotf[
                pl.ds(d * 4 + hq, 32, stride=16), :
            ].astype(BF)

    @pl.when(jnp.logical_not(last))
    def _():
        halo(2).start()

    @pl.when(jnp.logical_not(first))
    def _():
        halo(3).start()

    for load in loads[1:]:
        load.wait()
    f1f[104:128, :] = jnp.zeros((24, 16), F32)
    for tap in range(27):
        f1f[tap * 4 : tap * 4 + 4, :] = f1b[tap].astype(F32)

    lane = iota((64, 512), 1)
    group = iota((64, 512), 0)
    spread = (
        (lane % 16 == group % 16) & (lane // 256 == group // 32) & ((lane // 64) % 2 == (group // 16) % 2)
    ).astype(F32).astype(BF)
    picked = dot(chosen[...], f1f[...].astype(BF)).astype(BF)
    rows = jnp.concatenate([picked[g * 192 : (g + 1) * 192] for g in range(4)], axis=1)
    rows = dot(rows, spread)
    lane8 = iota((8, 512), 1)
    reach = iota((8, 512), 0) - (2 * ((lane8 // 16) % 4) + (lane8 // 128) % 2) + 1
    near = [reach == kh for kh in range(3)]
    matrix = jnp.zeros((64, 8, 512), F32)
    for kh in range(3):
        piece = rows[kh * 64 : (kh + 1) * 64].reshape(64, 1, 512)
        matrix = jnp.where(near[kh][None], piece, matrix)
    w1[...] = matrix.reshape(512, 512).T.astype(BF)

    tile4 = (iota((32, 128), 0) == iota((32, 128), 1) % 32).astype(F32).astype(BF)
    wide = dot(f2b[...], tile4)
    group4 = iota((16, 128), 1) // 32
    parts = []
    for kd in range(3):
        for kw in range(3):
            for hq in range(4):
                block = jnp.zeros((16, 128), F32)
                for kh in range(3):
                    if 0 <= hq - kh + 1 < 4:
                        tap = (kd * 3 + kh) * 3 + kw
                        block = jnp.where(group4 == hq - kh + 1, wide[tap * 16 : tap * 16 + 16], block)
                parts.append(block)
    joined = jnp.concatenate(parts, axis=0)
    w2t[...] = joined.astype(BF)
    w2[...] = joined.T.astype(BF)

    bias_one = column(b1b[...], 16)
    bias_two = column(b2b[...], 32)
    take = iota((256, 512), 1)
    sample = (iota((256, 512), 0) == 2 * (take % 128) - 1 + take // 128).astype(F32).astype(BF)

    def split_columns(part):
        source = raw[:, part * RIM : part * RIM + 64, :].reshape(256, 256)
        columns = dot(source, sample).reshape(4, 64, 512)[:, 8:56]
        for s in range(4):
            shifted[s * 4 : s * 4 + 4, part * RIM : part * RIM + RIM] = columns[
                :, :, s * 128 : (s + 1) * 128
            ].astype(BF)

    lane64 = iota((64, 128), 1)

    def window(p):
        return shifted[:, p * 16 : p * 16 + 32, :].reshape(512, LANES)

    def layer_one(pair):
        both = dot(w1[...], jnp.concatenate([window(p) for p in pair], axis=1))
        for n, p in enumerate(pair):
            linear = both[:, n * 128 : (n + 1) * 128].reshape(32, 16, LANES) + bias_one[None]
            linear = linear.reshape(8, 64, LANES)
            slope = jnp.where(linear > 0, 1.0, 0.3)
            if 2 <= p <= 5:
                slopes[p - 2] = slope
            mean = jnp.sum(linear * slope, axis=0) * 0.125
            if p < 2:
                mean = jnp.where(first, 0.0, mean)
            if p > 5:
                mean = jnp.where(last, 0.0, mean)
            base = p * 192
            pooled[base : base + 64, :] = jnp.where(
                lane64 == 0, 0.0, pltpu.roll(mean, 1, axis=1)
            ).astype(BF)
            pooled[base + 64 : base + 128, :] = mean.astype(BF)
            pooled[base + 128 : base + 192, :] = jnp.where(
                lane64 == 127, 0.0, pltpu.roll(mean, 127, axis=1)
            ).astype(BF)

    def layer_two(pair):
        both = dot(
            w2[...],
            jnp.concatenate([pooled[j * 192 : j * 192 + 576, :] for j in pair], axis=1),
        )
        for n, j in enumerate(pair):
            linear = both[:, n * 128 : (n + 1) * 128].reshape(4, 32, LANES)
            linear = (linear + bias_two[None]).reshape(128, LANES)
            slope = jnp.where(linear > 0, 1.0, 0.3)
            errors_two[j * 128 : (j + 1) * 128, :] = (
                cots[j * 128 : (j + 1) * 128, :].astype(F32) * slope
            ).astype(BF)
            if 1 <= j <= 4:
                out = linear * slope
                for hq in range(4):
                    cotf[pl.ds((j - 1) * 4 + hq, 32, stride=16), :] = out[hq * 32 : (hq + 1) * 32]

    split_columns(1)
    layer_one((3, 4))

    @pl.when(jnp.logical_not(first))
    def _():
        halo(0).wait_recv()

    split_columns(0)

    @pl.when(jnp.logical_not(last))
    def _():
        halo(1).wait_recv()

    split_columns(2)
    layer_one((2, 5))
    layer_one((1, 6))
    layer_one((0, 7))
    layer_two((2, 3))
    layer_two((1, 4))

    @pl.when(jnp.logical_not(first))
    def _():
        halo(2).wait_recv()

    @pl.when(jnp.logical_not(last))
    def _():
        halo(3).wait_recv()

    layer_two((0, 5))
    act_here[...] = cotf[...].astype(BF).reshape(32, 16, LANES)
    act_store = pltpu.make_async_copy(act_here, act_out, out_sem.at[0])
    act_store.start()

    own = jnp.concatenate(
        [errors_two[j * 128 : (j + 1) * 128, :] for j in range(1, 5)], axis=1
    )
    near_in = jnp.concatenate(
        [pooled[j * 192 : j * 192 + 576, :] for j in range(1, 5)], axis=1
    )
    near_in = jnp.concatenate([near_in, jnp.ones((16, 512), BF)], axis=0)
    outer = dot_nt(near_in, own)
    taps = []
    for kd in range(3):
        for kh in range(3):
            for kw in range(3):
                block = jnp.zeros((16, 128), F32)
                for hq in range(4):
                    if 0 <= hq - kh + 1 < 4:
                        at = ((kd * 3 + kw) * 4 + hq) * 16
                        block = jnp.where(group4 == hq - kh + 1, outer[at : at + 16], block)
                taps.append(fold(block, (64, 32)))
    taps.append(fold(outer[576:592], (64, 32)))
    for q in range(7):
        block = taps[4 * q]
        for slot in range(1, 4):
            block = jnp.where(group4 == slot, taps[4 * q + slot], block)
        terms[2 * q] = block[0:8]
        terms[2 * q + 1] = block[8:16]

    terms[14] = jnp.zeros((8, 128), F32)
    terms[15] = jnp.zeros((8, 128), F32)

    share = TILES // space_n

    def scatter(k):
        to = lax.rem(me + k, space_n)
        return pltpu.make_async_remote_copy(
            src_ref=terms.at[pl.ds(to * share, share)],
            dst_ref=landed.at[k - 1],
            send_sem=rs_send.at[k - 1],
            recv_sem=rs_recv.at[k - 1],
            device_id={"space": to},
            device_id_type=MESH,
        )

    def swap(axis, count, k, source, buffer, send, recv):
        return pltpu.make_async_remote_copy(
            src_ref=buffer.at[source],
            dst_ref=buffer.at[source],
            send_sem=send.at[k - 1],
            recv_sem=recv.at[k - 1],
            device_id={axis: lax.rem(lax.axis_index(axis) + k, count)},
            device_id_type=MESH,
        )

    def swap_start(axis, count, *where):
        for k in range(1, count):
            swap(axis, count, k, lax.axis_index(axis), *where).start()

    def swap_sent(axis, count, *where):
        for k in range(1, count):
            swap(axis, count, k, lax.axis_index(axis), *where).wait_send()

    def swap_landed(axis, count, *where):
        for k in range(1, count):
            source = lax.rem(lax.axis_index(axis) + count - k, count)
            swap(axis, count, k, source, *where).wait_recv()

    early_dp = ("dp", dp_n, across, dp_send, dp_recv)
    early_all = ("space", space_n, total, ag_send, ag_recv)
    last_space = ("space", space_n, late_space, ls_send, ls_recv)
    last_dp = ("dp", dp_n, late_dp, ld_send, ld_recv)

    for k in range(1, space_n):
        scatter(k).start()

    back = jnp.concatenate([w2t[kd * 192 : (kd + 1) * 192, :] for kd in (2, 1, 0)], axis=1)
    quad = dot(
        back,
        jnp.concatenate([errors_two[q * 128 : q * 128 + 384, :] for q in range(4)], axis=1),
    )
    for q in range(4):
        three = quad[:, q * 128 : (q + 1) * 128]
        grad = three[64:128]
        grad = grad + jnp.where(lane64 == 127, 0.0, pltpu.roll(three[0:64], 127, axis=1))
        grad = grad + jnp.where(lane64 == 0, 0.0, pltpu.roll(three[128:192], 1, axis=1))
        grad = grad.astype(BF).astype(F32)
        for hq in range(4):
            pgf[pl.ds(q * 4 + hq, 16, stride=16), :] = grad[hq * 16 : (hq + 1) * 16]
        errors_one[:, q * 128 : (q + 1) * 128] = (
            ((grad * 0.125)[None] * slopes[q]).astype(BF).reshape(512, LANES)
        )
    pg_here[...] = pgf[...].astype(BF).reshape(16, 16, LANES)
    pg_store = pltpu.make_async_copy(pg_here, pg_out, out_sem.at[1])
    pg_store.start()

    sums = terms[pl.ds(me * share, share)]
    for k in range(1, space_n):
        scatter(k).wait_recv()
        sums = sums + landed[k - 1]
    across[mine] = sums
    swap_start(*early_dp)

    near_in = jnp.concatenate([window(p) for p in range(2, 6)], axis=1)
    near_in = jnp.concatenate([near_in, jnp.ones((16, 512), BF)], axis=0)
    outer = dot_nt(near_in, errors_one[...])
    body = outer[0:512].reshape(4, 4, 4, 8, 512)
    low = iota((4, 3, 8, 128), 3) < 64
    for kh in range(3):
        summed = jnp.zeros((4, 4, 3, 8, 128), F32)
        for part in range(4):
            dd = part // 2
            cut = body[:, :, dd : dd + 3, :, part * 128 : (part + 1) * 128]
            mask = near[kh][:, part * 128 : (part + 1) * 128]
            summed = summed + jnp.where(mask[None, None, None], cut, 0.0)
        for kw in range(3):
            both = jnp.where(low, summed[kw], summed[kw + 1])
            for kd in range(3):
                tap = (kd * 3 + kh) * 3 + kw
                stack[tap * 32 : tap * 32 + 32, :] = both[:, kd].reshape(32, LANES)
    ones = outer[512:520]
    ones = ones[:, 0:128] + ones[:, 128:256] + ones[:, 256:384] + ones[:, 384:512]
    stack[864:872, :] = jnp.where(iota((8, 128), 0) == 0, ones, 0.0)
    stack[872:896, :] = jnp.zeros((24, 128), F32)
    gather = (iota((112, 896), 0) == iota((112, 896), 1) // 8).astype(F32).astype(BF)
    whole = stack[...]
    high = whole.astype(BF)
    rest = (whole - high.astype(F32)).astype(BF)
    reduced = fold(dot(gather, high) + dot(gather, rest), (64, 32, 16))
    group8 = iota((8, 128), 1) // 16
    for half in range(2):
        block = jnp.zeros((8, 128), F32)
        for slot in range(8):
            v = half * 8 + slot
            if v < 14:
                block = jnp.where(group8 == slot, reduced[v * 8 : v * 8 + 8], block)
        late[half] = block

    late_space[me] = late[...]
    swap_start(*last_space)

    swap_landed(*early_dp)
    sums = across[0]
    for k in range(1, dp_n):
        sums = sums + across[k]
    total[me] = sums
    swap_start(*early_all)

    swap_landed(*last_space)
    sums = late_space[0]
    for k in range(1, space_n):
        sums = sums + late_space[k]
    late_dp[mine] = sums
    swap_start(*last_dp)

    swap_landed(*early_all)
    sums_here[0:TILES] = total[...].reshape(TILES, 8, 128)
    swap_landed(*last_dp)
    sums = late_dp[0]
    for k in range(1, dp_n):
        sums = sums + late_dp[k]
    sums_here[TILES : TILES + 2] = sums
    sums_store = pltpu.make_async_copy(sums_here, sums_out, out_sem.at[2])
    sums_store.start()

    for k in range(1, space_n):
        scatter(k).wait_send()
    swap_sent(*early_dp)
    swap_sent(*early_all)
    swap_sent(*last_space)
    swap_sent(*last_dp)
    act_store.wait()
    pg_store.wait()
    sums_store.wait()

    @pl.when(jnp.logical_not(last))
    def _():
        halo(0).wait_send()
        halo(2).wait_send()

    @pl.when(jnp.logical_not(first))
    def _():
        halo(1).wait_send()
        halo(3).wait_send()


def finish(scale_one, scale_two, act, pg, sums_in, act_out, pg_out, g1_out, s1_out, g2_out, s2_out,
           sums_here, g1, s1, g2, s2, sem):
    load = pltpu.make_async_copy(sums_in, sums_here, sem.at[6])
    load.start()
    big = [
        pltpu.make_async_copy(act, act_out, sem.at[0]),
        pltpu.make_async_copy(pg, pg_out, sem.at[1]),
    ]
    for copy in big:
        copy.start()
    load.wait()
    sums = sums_here[...]
    for q in range(7):
        block = jnp.concatenate([sums[2 * q], sums[2 * q + 1]], axis=0) * scale_two
        for slot in range(4):
            tap = 4 * q + slot
            turned = block if slot == 0 else pltpu.roll(block, 128 - 32 * slot, axis=1)
            if tap < 27:
                g2[tap * 16 : tap * 16 + 16, :] = turned[:, 0:32]
            else:
                s2[...] = turned[0:1, 0:32]
    for v in range(14):
        block = sums[TILES + v // 8] * scale_one
        slot = v % 8
        turned = block if slot == 0 else pltpu.roll(block, 128 - 16 * slot, axis=1)
        g1[2 * v] = turned[0:4, 0:16]
        if v < 13:
            g1[2 * v + 1] = turned[4:8, 0:16]
        else:
            s1[...] = turned[4:5, 0:16]
    small = [
        pltpu.make_async_copy(src, dst, sem.at[2 + n])
        for n, (src, dst) in enumerate(((g1, g1_out), (s1, s1_out), (g2, g2_out), (s2, s2_out)))
    ]
    for copy in small:
        copy.start()
    for copy in big + small:
        copy.wait()


def shards(dp_n, space_n, volume, first_filters, first_biases, second_filters, second_biases, cotangent):
    _, c_in, planes, high, wide = volume.shape
    c1, c2 = first_filters.shape[0], second_filters.shape[0]
    assert (c_in, planes, high, wide, c1, c2) == (4, 8, 8, 256, 16, 32)
    assert TILES % space_n == 0
    count_one = dp_n * space_n * planes * high * wide
    scale_one = 1.0 / math.sqrt(count_one)
    scale_two = 1.0 / math.sqrt(count_one / 8)
    share = TILES // space_n
    f1 = first_filters.transpose(2, 3, 4, 1, 0).reshape(27, 4, 16)
    f2 = second_filters.transpose(2, 3, 4, 1, 0).reshape(432, 32)
    vmem = pl.BlockSpec(memory_space=pltpu.VMEM)
    hbm = pl.BlockSpec(memory_space=pltpu.HBM)
    dma = pltpu.SemaphoreType.DMA
    act, pg, sums = pl.pallas_call(
        functools.partial(kernel, dp_n, space_n),
        out_shape=(
            jax.ShapeDtypeStruct((32, 16, 128), BF),
            jax.ShapeDtypeStruct((16, 16, 128), BF),
            jax.ShapeDtypeStruct((TILES + 2, 8, 128), F32),
        ),
        in_specs=[hbm] * 7,
        out_specs=(hbm,) * 3,
        scratch_shapes=[
            pltpu.VMEM((4, 2 * RIM + 64, 256), BF),
            pltpu.VMEM((32, 16, 128), BF),
            pltpu.VMEM((27, 4, 16), BF),
            pltpu.VMEM((128, 16), F32),
            pltpu.VMEM((432, 32), BF),
            pltpu.VMEM((1, 16), F32),
            pltpu.VMEM((1, 32), F32),
            pltpu.VMEM((768, 128), BF),
            pltpu.VMEM((768, 128), BF),
            pltpu.VMEM((512, 128), F32),
            pltpu.VMEM((16, 144, 128), BF),
            pltpu.VMEM((8 * 192, 128), BF),
            pltpu.VMEM((4, 8, 64, 128), F32),
            pltpu.VMEM((768, 128), BF),
            pltpu.VMEM((512, 512), BF),
            pltpu.VMEM((256, 128), F32),
            pltpu.VMEM((512, 512), BF),
            pltpu.VMEM((128, 576), BF),
            pltpu.VMEM((576, 128), BF),
            pltpu.VMEM((896, 128), F32),
            pltpu.VMEM((TILES, 8, 128), F32),
            pltpu.VMEM((space_n - 1, share, 8, 128), F32),
            pltpu.VMEM((dp_n, share, 8, 128), F32),
            pltpu.VMEM((space_n, share, 8, 128), F32),
            pltpu.VMEM((2, 8, 128), F32),
            pltpu.VMEM((space_n, 2, 8, 128), F32),
            pltpu.VMEM((dp_n, 2, 8, 128), F32),
            pltpu.VMEM((32, 16, 128), BF),
            pltpu.VMEM((16, 16, 128), BF),
            pltpu.VMEM((TILES + 2, 8, 128), F32),
            dma((3,)),
            dma((7,)),
            dma((4,)),
            dma((4,)),
        ]
        + [dma((space_n - 1,))] * 2
        + [dma((dp_n - 1,))] * 2
        + [dma((space_n - 1,))] * 4
        + [dma((dp_n - 1,))] * 2,
        compiler_params=pltpu.CompilerParams(
            collective_id=0, has_side_effects=True, vmem_limit_bytes=VMEM_LIMIT
        ),
    )(
        volume.reshape(4, 64, 256),
        cotangent.reshape(32, 16, 128),
        f1,
        f2,
        first_biases.reshape(1, 16),
        second_biases.reshape(1, 32),
        jnp.asarray(tap_choice(), BF),
    )
    act, pg, g1, s1, g2, s2 = pl.pallas_call(
        functools.partial(finish, scale_one, scale_two),
        out_shape=(
            jax.ShapeDtypeStruct((32, 16, 128), BF),
            jax.ShapeDtypeStruct((16, 16, 128), BF),
            jax.ShapeDtypeStruct((27, 4, 16), F32),
            jax.ShapeDtypeStruct((1, 16), F32),
            jax.ShapeDtypeStruct((432, 32), F32),
            jax.ShapeDtypeStruct((1, 32), F32),
        ),
        in_specs=[hbm] * 3,
        out_specs=(hbm,) * 6,
        scratch_shapes=[
            pltpu.VMEM((TILES + 2, 8, 128), F32),
            pltpu.VMEM((27, 4, 16), F32),
            pltpu.VMEM((1, 16), F32),
            pltpu.VMEM((432, 32), F32),
            pltpu.VMEM((1, 32), F32),
            dma((7,)),
        ],
        compiler_params=pltpu.CompilerParams(vmem_limit_bytes=VMEM_LIMIT),
    )(act, pg, sums)
    return (
        act.reshape(1, 32, 4, 4, 128),
        pg.reshape(1, 16, 4, 4, 128),
        g1.reshape(3, 3, 3, 4, 16).transpose(4, 3, 0, 1, 2),
        s1.reshape(16),
        g2.reshape(3, 3, 3, 16, 32).transpose(4, 3, 0, 1, 2),
        s2.reshape(32),
    )


def solution(mesh):
    placed = (
        P("dp", None, "space", None, None),
        P(),
        P(),
        P(),
        P(),
        P("dp", None, "space", None, None),
    )
    return jax.shard_map(
        functools.partial(shards, mesh.shape["dp"], mesh.shape["space"]),
        mesh=mesh,
        in_specs=placed,
        out_specs=(
            P("dp", None, "space", None, None),
            P("dp", None, "space", None, None),
            P(),
            P(),
            P(),
            P(),
        ),
        check_vma=False,
    )
```

```python
import functools
import math

import jax
import jax.numpy as jnp
import numpy as np
from jax import lax
from jax.experimental import pallas as pl
from jax.experimental.pallas import tpu as pltpu
from jax.sharding import PartitionSpec as P

BF = jnp.bfloat16
F32 = jnp.float32
MESH = pl.DeviceIdType.MESH
LANES = 128
RIM = 48
VMEM_LIMIT = 60 * 1024 * 1024
TILES = 16


def tap_choice():
    table = np.zeros((2, 2, 3, 4, 4, 4, 128), np.float32)
    for dd in range(2):
        for wpar in range(2):
            for kh in range(3):
                for s in range(4):
                    for dz in range(4):
                        kd, kw = dz - dd, s - wpar
                        if 0 <= kd < 3 and 0 <= kw < 3:
                            for i in range(4):
                                table[dd, wpar, kh, s, i, dz, ((kd * 3 + kh) * 3 + kw) * 4 + i] = 1
    return table.reshape(4 * 192, 128)


def iota(shape, dim):
    return lax.broadcasted_iota(jnp.int32, shape, dim)


def dot(a, b):
    return jnp.dot(a, b, preferred_element_type=F32)


def dot_nt(a, b):
    return lax.dot_general(a, b, (((1,), (1,)), ((), ())), preferred_element_type=F32)


def column(row, count):
    return jnp.sum(
        jnp.where(iota((count, count), 0) == iota((count, count), 1), row, 0.0),
        axis=1,
        keepdims=True,
    )


def fold(values, steps):
    for step in steps:
        values = values + pltpu.roll(values, step, axis=values.ndim - 1)
    return values


def kernel(
    dp_n, space_n,
    vol, cot, f1, f2, b1, b2, choice,
    act_out, pg_out, sums_out,
    raw, cotb, f1b, f1f, f2b, b1b, b2b, chosen,
    cots, cotf, shifted, pooled, slopes, errors_two, errors_one, pgf, w1, w2, w2t,
    stack, terms, landed, across, total, late, late_space, late_dp,
    act_here, pg_here, sums_here, out_sem, in_sem, halo_send, halo_recv, rs_send, rs_recv, dp_send, dp_recv, ag_send, ag_recv,
    ls_send, ls_recv, ld_send, ld_recv,
):
    me = lax.axis_index("space")
    mine = lax.axis_index("dp")
    first = me == 0
    last = me == space_n - 1

    barrier = pltpu.get_barrier_semaphore()
    for k in range(1, space_n):
        pl.semaphore_signal(
            barrier, inc=1, device_id={"space": lax.rem(me + k, space_n)}, device_id_type=MESH
        )
    for k in range(1, dp_n):
        pl.semaphore_signal(
            barrier, inc=1, device_id={"dp": lax.rem(mine + k, dp_n)}, device_id_type=MESH
        )
    loads = [
        pltpu.make_async_copy(src, dst, in_sem.at[n])
        for n, (src, dst) in enumerate(
            (
                (cot, cotb),
                (f1, f1b),
                (choice, chosen),
                (f2, f2b),
                (b1, b1b),
                (b2, b2b),
                (vol, raw.at[:, RIM : RIM + 64]),
            )
        )
    ]
    for load in loads:
        load.start()

    @pl.when(first)
    def _():
        raw[:, 0:RIM, :] = jnp.zeros((4, RIM, 256), BF)
        cots[0:128, :] = jnp.zeros((128, LANES), BF)

    @pl.when(last)
    def _():
        raw[:, RIM + 64 :, :] = jnp.zeros((4, RIM, 256), BF)
        cots[640:768, :] = jnp.zeros((128, LANES), BF)

    right = lax.rem(me + 1, space_n)
    left = lax.rem(me + space_n - 1, space_n)

    def halo(which):
        src, dst, to = (
            (vol.at[:, 16:64], raw.at[:, 0:RIM], right),
            (vol.at[:, 0:RIM], raw.at[:, RIM + 64 : 2 * RIM + 64], left),
            (cots.at[512:640], cots.at[0:128], right),
            (cots.at[128:256], cots.at[640:768], left),
        )[which]
        return pltpu.make_async_remote_copy(
            src_ref=src,
            dst_ref=dst,
            send_sem=halo_send.at[which],
            recv_sem=halo_recv.at[which],
            device_id={"space": to},
            device_id_type=MESH,
        )

    pl.semaphore_wait(barrier, space_n - 1 + dp_n - 1)

    @pl.when(jnp.logical_not(last))
    def _():
        halo(0).start()

    @pl.when(jnp.logical_not(first))
    def _():
        halo(1).start()

    loads[0].wait()
    cotf[...] = cotb[...].reshape(512, LANES).astype(F32)
    for d in range(4):
        for hq in range(4):
            cots[pl.ds((1 + d) * 128 + hq * 32, 32), :] = cotf[
                pl.ds(d * 4 + hq, 32, stride=16), :
            ].astype(BF)

    @pl.when(jnp.logical_not(last))
    def _():
        halo(2).start()

    @pl.when(jnp.logical_not(first))
    def _():
        halo(3).start()

    for load in loads[1:]:
        load.wait()
    f1f[104:128, :] = jnp.zeros((24, 16), F32)
    for tap in range(27):
        f1f[tap * 4 : tap * 4 + 4, :] = f1b[tap].astype(F32)

    lane = iota((64, 512), 1)
    group = iota((64, 512), 0)
    spread = (
        (lane % 16 == group % 16) & (lane // 256 == group // 32) & ((lane // 64) % 2 == (group // 16) % 2)
    ).astype(F32).astype(BF)
    picked = dot(chosen[...], f1f[...].astype(BF)).astype(BF)
    rows = jnp.concatenate([picked[g * 192 : (g + 1) * 192] for g in range(4)], axis=1)
    rows = dot(rows, spread)
    lane8 = iota((8, 512), 1)
    reach = iota((8, 512), 0) - (2 * ((lane8 // 16) % 4) + (lane8 // 128) % 2) + 1
    near = [reach == kh for kh in range(3)]
    matrix = jnp.zeros((64, 8, 512), F32)
    for kh in range(3):
        piece = rows[kh * 64 : (kh + 1) * 64].reshape(64, 1, 512)
        matrix = jnp.where(near[kh][None], piece, matrix)
    w1[...] = matrix.reshape(512, 512).T.astype(BF)

    tile4 = (iota((32, 128), 0) == iota((32, 128), 1) % 32).astype(F32).astype(BF)
    wide = dot(f2b[...], tile4)
    group4 = iota((16, 128), 1) // 32
    parts = []
    for kd in range(3):
        for kw in range(3):
            for hq in range(4):
                block = jnp.zeros((16, 128), F32)
                for kh in range(3):
                    if 0 <= hq - kh + 1 < 4:
                        tap = (kd * 3 + kh) * 3 + kw
                        block = jnp.where(group4 == hq - kh + 1, wide[tap * 16 : tap * 16 + 16], block)
                parts.append(block)
    joined = jnp.concatenate(parts, axis=0)
    w2t[...] = joined.astype(BF)
    w2[...] = joined.T.astype(BF)

    bias_one = column(b1b[...], 16)
    bias_two = column(b2b[...], 32)
    take = iota((256, 512), 1)
    sample = (iota((256, 512), 0) == 2 * (take % 128) - 1 + take // 128).astype(F32).astype(BF)

    def split_columns(part):
        source = raw[:, part * RIM : part * RIM + 64, :].reshape(256, 256)
        columns = dot(source, sample).reshape(4, 64, 512)[:, 8:56]
        for s in range(4):
            shifted[s * 4 : s * 4 + 4, part * RIM : part * RIM + RIM] = columns[
                :, :, s * 128 : (s + 1) * 128
            ].astype(BF)

    lane64 = iota((64, 128), 1)

    def window(p):
        return shifted[:, p * 16 : p * 16 + 32, :].reshape(512, LANES)

    def layer_one(pair):
        both = dot(w1[...], jnp.concatenate([window(p) for p in pair], axis=1))
        for n, p in enumerate(pair):
            linear = both[:, n * 128 : (n + 1) * 128].reshape(32, 16, LANES) + bias_one[None]
            linear = linear.reshape(8, 64, LANES)
            slope = jnp.where(linear > 0, 1.0, 0.3)
            if 2 <= p <= 5:
                slopes[p - 2] = slope
            mean = jnp.sum(linear * slope, axis=0) * 0.125
            if p < 2:
                mean = jnp.where(first, 0.0, mean)
            if p > 5:
                mean = jnp.where(last, 0.0, mean)
            base = p * 192
            pooled[base : base + 64, :] = jnp.where(
                lane64 == 0, 0.0, pltpu.roll(mean, 1, axis=1)
            ).astype(BF)
            pooled[base + 64 : base + 128, :] = mean.astype(BF)
            pooled[base + 128 : base + 192, :] = jnp.where(
                lane64 == 127, 0.0, pltpu.roll(mean, 127, axis=1)
            ).astype(BF)

    def layer_two(pair):
        both = dot(
            w2[...],
            jnp.concatenate([pooled[j * 192 : j * 192 + 576, :] for j in pair], axis=1),
        )
        for n, j in enumerate(pair):
            linear = both[:, n * 128 : (n + 1) * 128].reshape(4, 32, LANES)
            linear = (linear + bias_two[None]).reshape(128, LANES)
            slope = jnp.where(linear > 0, 1.0, 0.3)
            errors_two[j * 128 : (j + 1) * 128, :] = (
                cots[j * 128 : (j + 1) * 128, :].astype(F32) * slope
            ).astype(BF)
            if 1 <= j <= 4:
                out = linear * slope
                for hq in range(4):
                    cotf[pl.ds((j - 1) * 4 + hq, 32, stride=16), :] = out[hq * 32 : (hq + 1) * 32]

    split_columns(1)
    layer_one((3, 4))

    @pl.when(jnp.logical_not(first))
    def _():
        halo(0).wait_recv()

    split_columns(0)

    @pl.when(jnp.logical_not(last))
    def _():
        halo(1).wait_recv()

    split_columns(2)
    layer_one((2, 5))
    layer_one((1, 6))
    layer_one((0, 7))
    layer_two((2, 3))
    layer_two((1, 4))

    @pl.when(jnp.logical_not(first))
    def _():
        halo(2).wait_recv()

    @pl.when(jnp.logical_not(last))
    def _():
        halo(3).wait_recv()

    layer_two((0, 5))
    act_here[...] = cotf[...].astype(BF).reshape(32, 16, LANES)
    act_store = pltpu.make_async_copy(act_here, act_out, out_sem.at[0])
    act_store.start()

    own = jnp.concatenate(
        [errors_two[j * 128 : (j + 1) * 128, :] for j in range(1, 5)], axis=1
    )
    near_in = jnp.concatenate(
        [pooled[j * 192 : j * 192 + 576, :] for j in range(1, 5)], axis=1
    )
    near_in = jnp.concatenate([near_in, jnp.ones((16, 512), BF)], axis=0)
    outer = dot_nt(near_in, own)
    taps = []
    for kd in range(3):
        for kh in range(3):
            for kw in range(3):
                block = jnp.zeros((16, 128), F32)
                for hq in range(4):
                    if 0 <= hq - kh + 1 < 4:
                        at = ((kd * 3 + kw) * 4 + hq) * 16
                        block = jnp.where(group4 == hq - kh + 1, outer[at : at + 16], block)
                taps.append(fold(block, (64, 32)))
    taps.append(fold(outer[576:592], (64, 32)))
    for q in range(7):
        block = taps[4 * q]
        for slot in range(1, 4):
            block = jnp.where(group4 == slot, taps[4 * q + slot], block)
        terms[2 * q] = block[0:8]
        terms[2 * q + 1] = block[8:16]

    terms[14] = jnp.zeros((8, 128), F32)
    terms[15] = jnp.zeros((8, 128), F32)

    share = TILES // space_n

    def scatter(k):
        to = lax.rem(me + k, space_n)
        return pltpu.make_async_remote_copy(
            src_ref=terms.at[pl.ds(to * share, share)],
            dst_ref=landed.at[k - 1],
            send_sem=rs_send.at[k - 1],
            recv_sem=rs_recv.at[k - 1],
            device_id={"space": to},
            device_id_type=MESH,
        )

    def swap(axis, count, k, source, buffer, send, recv):
        return pltpu.make_async_remote_copy(
            src_ref=buffer.at[source],
            dst_ref=buffer.at[source],
            send_sem=send.at[k - 1],
            recv_sem=recv.at[k - 1],
            device_id={axis: lax.rem(lax.axis_index(axis) + k, count)},
            device_id_type=MESH,
        )

    def swap_start(axis, count, *where):
        for k in range(1, count):
            swap(axis, count, k, lax.axis_index(axis), *where).start()

    def swap_sent(axis, count, *where):
        for k in range(1, count):
            swap(axis, count, k, lax.axis_index(axis), *where).wait_send()

    def swap_landed(axis, count, *where):
        for k in range(1, count):
            source = lax.rem(lax.axis_index(axis) + count - k, count)
            swap(axis, count, k, source, *where).wait_recv()

    early_dp = ("dp", dp_n, across, dp_send, dp_recv)
    early_all = ("space", space_n, total, ag_send, ag_recv)
    last_space = ("space", space_n, late_space, ls_send, ls_recv)
    last_dp = ("dp", dp_n, late_dp, ld_send, ld_recv)

    back = jnp.concatenate([w2t[kd * 192 : (kd + 1) * 192, :] for kd in (2, 1, 0)], axis=1)
    quad = dot(
        back,
        jnp.concatenate([errors_two[q * 128 : q * 128 + 384, :] for q in range(4)], axis=1),
    )
    for q in range(4):
        three = quad[:, q * 128 : (q + 1) * 128]
        grad = three[64:128]
        grad = grad + jnp.where(lane64 == 127, 0.0, pltpu.roll(three[0:64], 127, axis=1))
        grad = grad + jnp.where(lane64 == 0, 0.0, pltpu.roll(three[128:192], 1, axis=1))
        grad = grad.astype(BF).astype(F32)
        for hq in range(4):
            pgf[pl.ds(q * 4 + hq, 16, stride=16), :] = grad[hq * 16 : (hq + 1) * 16]
        errors_one[:, q * 128 : (q + 1) * 128] = (
            ((grad * 0.125)[None] * slopes[q]).astype(BF).reshape(512, LANES)
        )
    pg_here[...] = pgf[...].astype(BF).reshape(16, 16, LANES)
    pg_store = pltpu.make_async_copy(pg_here, pg_out, out_sem.at[1])
    pg_store.start()

    for k in range(1, space_n):
        scatter(k).start()

    near_in = jnp.concatenate([window(p) for p in range(2, 6)], axis=1)
    near_in = jnp.concatenate([near_in, jnp.ones((16, 512), BF)], axis=0)
    outer = dot_nt(near_in, errors_one[...])
    body = outer[0:512].reshape(4, 4, 4, 8, 512)
    low = iota((4, 3, 8, 128), 3) < 64
    for kh in range(3):
        summed = jnp.zeros((4, 4, 3, 8, 128), F32)
        for part in range(4):
            dd = part // 2
            cut = body[:, :, dd : dd + 3, :, part * 128 : (part + 1) * 128]
            mask = near[kh][:, part * 128 : (part + 1) * 128]
            summed = summed + jnp.where(mask[None, None, None], cut, 0.0)
        for kw in range(3):
            both = jnp.where(low, summed[kw], summed[kw + 1])
            for kd in range(3):
                tap = (kd * 3 + kh) * 3 + kw
                stack[tap * 32 : tap * 32 + 32, :] = both[:, kd].reshape(32, LANES)
    ones = outer[512:520]
    ones = ones[:, 0:128] + ones[:, 128:256] + ones[:, 256:384] + ones[:, 384:512]
    stack[864:872, :] = jnp.where(iota((8, 128), 0) == 0, ones, 0.0)
    stack[872:896, :] = jnp.zeros((24, 128), F32)
    gather = (iota((112, 896), 0) == iota((112, 896), 1) // 8).astype(F32).astype(BF)
    whole = stack[...]
    high = whole.astype(BF)
    rest = (whole - high.astype(F32)).astype(BF)
    reduced = fold(dot(gather, high) + dot(gather, rest), (64, 32, 16))
    group8 = iota((8, 128), 1) // 16
    for half in range(2):
        block = jnp.zeros((8, 128), F32)
        for slot in range(8):
            v = half * 8 + slot
            if v < 14:
                block = jnp.where(group8 == slot, reduced[v * 8 : v * 8 + 8], block)
        late[half] = block

    late_space[me] = late[...]
    swap_start(*last_space)

    sums = terms[pl.ds(me * share, share)]
    for k in range(1, space_n):
        scatter(k).wait_recv()
        sums = sums + landed[k - 1]
    across[mine] = sums
    swap_start(*early_dp)

    swap_landed(*last_space)
    sums = late_space[0]
    for k in range(1, space_n):
        sums = sums + late_space[k]
    late_dp[mine] = sums
    swap_start(*last_dp)

    swap_landed(*early_dp)
    sums = across[0]
    for k in range(1, dp_n):
        sums = sums + across[k]
    total[me] = sums
    swap_start(*early_all)

    swap_landed(*early_all)
    sums_here[0:TILES] = total[...].reshape(TILES, 8, 128)
    swap_landed(*last_dp)
    sums = late_dp[0]
    for k in range(1, dp_n):
        sums = sums + late_dp[k]
    sums_here[TILES : TILES + 2] = sums
    sums_store = pltpu.make_async_copy(sums_here, sums_out, out_sem.at[2])
    sums_store.start()

    for k in range(1, space_n):
        scatter(k).wait_send()
    swap_sent(*early_dp)
    swap_sent(*early_all)
    swap_sent(*last_space)
    swap_sent(*last_dp)
    act_store.wait()
    pg_store.wait()
    sums_store.wait()

    @pl.when(jnp.logical_not(last))
    def _():
        halo(0).wait_send()
        halo(2).wait_send()

    @pl.when(jnp.logical_not(first))
    def _():
        halo(1).wait_send()
        halo(3).wait_send()


def finish(scale_one, scale_two, act, pg, sums_in, act_out, pg_out, g1_out, s1_out, g2_out, s2_out,
           act_here, pg_here, sums_here, g1, s1, g2, s2, sem):
    load = pltpu.make_async_copy(sums_in, sums_here, sem.at[6])
    load.start()
    loads = [
        pltpu.make_async_copy(act, act_here, sem.at[7]),
        pltpu.make_async_copy(pg, pg_here, sem.at[8]),
    ]
    for copy in loads:
        copy.start()
    big = [
        pltpu.make_async_copy(act_here, act_out, sem.at[0]),
        pltpu.make_async_copy(pg_here, pg_out, sem.at[1]),
    ]
    for ready, copy in zip(loads, big):
        ready.wait()
        copy.start()
    load.wait()
    sums = sums_here[...]
    for q in range(7):
        block = jnp.concatenate([sums[2 * q], sums[2 * q + 1]], axis=0) * scale_two
        for slot in range(4):
            tap = 4 * q + slot
            turned = block if slot == 0 else pltpu.roll(block, 128 - 32 * slot, axis=1)
            if tap < 27:
                g2[tap * 16 : tap * 16 + 16, :] = turned[:, 0:32]
            else:
                s2[...] = turned[0:1, 0:32]
    for v in range(14):
        block = sums[TILES + v // 8] * scale_one
        slot = v % 8
        turned = block if slot == 0 else pltpu.roll(block, 128 - 16 * slot, axis=1)
        g1[2 * v] = turned[0:4, 0:16]
        if v < 13:
            g1[2 * v + 1] = turned[4:8, 0:16]
        else:
            s1[...] = turned[4:5, 0:16]
    small = [
        pltpu.make_async_copy(src, dst, sem.at[2 + n])
        for n, (src, dst) in enumerate(((g1, g1_out), (s1, s1_out), (g2, g2_out), (s2, s2_out)))
    ]
    for copy in small:
        copy.start()
    for copy in big + small:
        copy.wait()


def shards(dp_n, space_n, volume, first_filters, first_biases, second_filters, second_biases, cotangent):
    _, c_in, planes, high, wide = volume.shape
    c1, c2 = first_filters.shape[0], second_filters.shape[0]
    assert (c_in, planes, high, wide, c1, c2) == (4, 8, 8, 256, 16, 32)
    assert TILES % space_n == 0
    count_one = dp_n * space_n * planes * high * wide
    scale_one = 1.0 / math.sqrt(count_one)
    scale_two = 1.0 / math.sqrt(count_one / 8)
    share = TILES // space_n
    f1 = first_filters.transpose(2, 3, 4, 1, 0).reshape(27, 4, 16)
    f2 = second_filters.transpose(2, 3, 4, 1, 0).reshape(432, 32)
    vmem = pl.BlockSpec(memory_space=pltpu.VMEM)
    hbm = pl.BlockSpec(memory_space=pltpu.HBM)
    dma = pltpu.SemaphoreType.DMA
    act, pg, sums = pl.pallas_call(
        functools.partial(kernel, dp_n, space_n),
        out_shape=(
            jax.ShapeDtypeStruct((32, 16, 128), BF),
            jax.ShapeDtypeStruct((16, 16, 128), BF),
            jax.ShapeDtypeStruct((TILES + 2, 8, 128), F32),
        ),
        in_specs=[hbm] * 7,
        out_specs=(hbm,) * 3,
        scratch_shapes=[
            pltpu.VMEM((4, 2 * RIM + 64, 256), BF),
            pltpu.VMEM((32, 16, 128), BF),
            pltpu.VMEM((27, 4, 16), BF),
            pltpu.VMEM((128, 16), F32),
            pltpu.VMEM((432, 32), BF),
            pltpu.VMEM((1, 16), F32),
            pltpu.VMEM((1, 32), F32),
            pltpu.VMEM((768, 128), BF),
            pltpu.VMEM((768, 128), BF),
            pltpu.VMEM((512, 128), F32),
            pltpu.VMEM((16, 144, 128), BF),
            pltpu.VMEM((8 * 192, 128), BF),
            pltpu.VMEM((4, 8, 64, 128), F32),
            pltpu.VMEM((768, 128), BF),
            pltpu.VMEM((512, 512), BF),
            pltpu.VMEM((256, 128), F32),
            pltpu.VMEM((512, 512), BF),
            pltpu.VMEM((128, 576), BF),
            pltpu.VMEM((576, 128), BF),
            pltpu.VMEM((896, 128), F32),
            pltpu.VMEM((TILES, 8, 128), F32),
            pltpu.VMEM((space_n - 1, share, 8, 128), F32),
            pltpu.VMEM((dp_n, share, 8, 128), F32),
            pltpu.VMEM((space_n, share, 8, 128), F32),
            pltpu.VMEM((2, 8, 128), F32),
            pltpu.VMEM((space_n, 2, 8, 128), F32),
            pltpu.VMEM((dp_n, 2, 8, 128), F32),
            pltpu.VMEM((32, 16, 128), BF),
            pltpu.VMEM((16, 16, 128), BF),
            pltpu.VMEM((TILES + 2, 8, 128), F32),
            dma((3,)),
            dma((7,)),
            dma((4,)),
            dma((4,)),
        ]
        + [dma((space_n - 1,))] * 2
        + [dma((dp_n - 1,))] * 2
        + [dma((space_n - 1,))] * 4
        + [dma((dp_n - 1,))] * 2,
        compiler_params=pltpu.CompilerParams(
            collective_id=0, has_side_effects=True, vmem_limit_bytes=VMEM_LIMIT
        ),
    )(
        volume.reshape(4, 64, 256),
        cotangent.reshape(32, 16, 128),
        f1,
        f2,
        first_biases.reshape(1, 16),
        second_biases.reshape(1, 32),
        jnp.asarray(tap_choice(), BF),
    )
    act, pg, g1, s1, g2, s2 = pl.pallas_call(
        functools.partial(finish, scale_one, scale_two),
        out_shape=(
            jax.ShapeDtypeStruct((32, 16, 128), BF),
            jax.ShapeDtypeStruct((16, 16, 128), BF),
            jax.ShapeDtypeStruct((27, 4, 16), F32),
            jax.ShapeDtypeStruct((1, 16), F32),
            jax.ShapeDtypeStruct((432, 32), F32),
            jax.ShapeDtypeStruct((1, 32), F32),
        ),
        in_specs=[hbm] * 3,
        out_specs=(hbm,) * 6,
        scratch_shapes=[
            pltpu.VMEM((32, 16, 128), BF),
            pltpu.VMEM((16, 16, 128), BF),
            pltpu.VMEM((TILES + 2, 8, 128), F32),
            pltpu.VMEM((27, 4, 16), F32),
            pltpu.VMEM((1, 16), F32),
            pltpu.VMEM((432, 32), F32),
            pltpu.VMEM((1, 32), F32),
            dma((9,)),
        ],
        compiler_params=pltpu.CompilerParams(vmem_limit_bytes=VMEM_LIMIT),
    )(act, pg, sums)
    return (
        act.reshape(1, 32, 4, 4, 128),
        pg.reshape(1, 16, 4, 4, 128),
        g1.reshape(3, 3, 3, 4, 16).transpose(4, 3, 0, 1, 2),
        s1.reshape(16),
        g2.reshape(3, 3, 3, 16, 32).transpose(4, 3, 0, 1, 2),
        s2.reshape(32),
    )


def solution(mesh):
    placed = (
        P("dp", None, "space", None, None),
        P(),
        P(),
        P(),
        P(),
        P("dp", None, "space", None, None),
    )
    return jax.shard_map(
        functools.partial(shards, mesh.shape["dp"], mesh.shape["space"]),
        mesh=mesh,
        in_specs=placed,
        out_specs=(
            P("dp", None, "space", None, None),
            P("dp", None, "space", None, None),
            P(),
            P(),
            P(),
            P(),
        ),
        check_vma=False,
    )
```

```python
import functools
import math

import jax
import jax.numpy as jnp
import numpy as np
from jax import lax
from jax.experimental import pallas as pl
from jax.experimental.pallas import tpu as pltpu
from jax.sharding import PartitionSpec as P

BF = jnp.bfloat16
F32 = jnp.float32
MESH = pl.DeviceIdType.MESH
LANES = 128
RIM = 32
VMEM_LIMIT = 60 * 1024 * 1024
TILES = 16


def tap_choice():
    table = np.zeros((2, 2, 3, 4, 4, 4, 128), np.float32)
    for dd in range(2):
        for wpar in range(2):
            for kh in range(3):
                for s in range(4):
                    for dz in range(4):
                        kd, kw = dz - dd, s - wpar
                        if 0 <= kd < 3 and 0 <= kw < 3:
                            for i in range(4):
                                table[dd, wpar, kh, s, i, dz, ((kd * 3 + kh) * 3 + kw) * 4 + i] = 1
    return table.reshape(4 * 192, 128)


def iota(shape, dim):
    return lax.broadcasted_iota(jnp.int32, shape, dim)


def dot(a, b):
    return jnp.dot(a, b, preferred_element_type=F32)


def dot_nt(a, b):
    return lax.dot_general(a, b, (((1,), (1,)), ((), ())), preferred_element_type=F32)


def column(row, count):
    return jnp.sum(
        jnp.where(iota((count, count), 0) == iota((count, count), 1), row, 0.0),
        axis=1,
        keepdims=True,
    )


def fold(values, steps):
    for step in steps:
        values = values + pltpu.roll(values, step, axis=values.ndim - 1)
    return values


def kernel(
    dp_n, space_n,
    vol, cot, f1, f2, b1, b2, choice,
    act_out, pg_out, sums_out,
    raw, cotb, f1b, f1f, f2b, b1b, b2b, chosen,
    cots, cotf, shifted, pooled, slopes, errors_two, errors_one, pgf, w1, w2, w2t,
    stack, terms, landed, across, total, late, late_space, late_dp,
    act_here, pg_here, sums_here, out_sem, in_sem, halo_send, halo_recv, rs_send, rs_recv, dp_send, dp_recv, ag_send, ag_recv,
    ls_send, ls_recv, ld_send, ld_recv,
):
    me = lax.axis_index("space")
    mine = lax.axis_index("dp")
    first = me == 0
    last = me == space_n - 1

    barrier = pltpu.get_barrier_semaphore()
    for k in range(1, space_n):
        pl.semaphore_signal(
            barrier, inc=1, device_id={"space": lax.rem(me + k, space_n)}, device_id_type=MESH
        )
    for k in range(1, dp_n):
        pl.semaphore_signal(
            barrier, inc=1, device_id={"dp": lax.rem(mine + k, dp_n)}, device_id_type=MESH
        )
    loads = [
        pltpu.make_async_copy(src, dst, in_sem.at[n])
        for n, (src, dst) in enumerate(
            (
                (cot, cotb),
                (f1, f1b),
                (choice, chosen),
                (f2, f2b),
                (b1, b1b),
                (b2, b2b),
                (vol, raw.at[:, RIM : RIM + 64]),
            )
        )
    ]
    for load in loads:
        load.start()

    @pl.when(first)
    def _():
        raw[:, 0:RIM, :] = jnp.zeros((4, RIM, 256), BF)
        errors_two[0:128, :] = jnp.zeros((128, LANES), BF)

    @pl.when(last)
    def _():
        raw[:, RIM + 64 :, :] = jnp.zeros((4, RIM, 256), BF)
        errors_two[640:768, :] = jnp.zeros((128, LANES), BF)

    right = lax.rem(me + 1, space_n)
    left = lax.rem(me + space_n - 1, space_n)

    def halo(which):
        src, dst, to = (
            (vol.at[:, 64 - RIM : 64], raw.at[:, 0:RIM], right),
            (vol.at[:, 0:RIM], raw.at[:, RIM + 64 : 2 * RIM + 64], left),
            (errors_two.at[512:640], errors_two.at[0:128], right),
            (errors_two.at[128:256], errors_two.at[640:768], left),
        )[which]
        return pltpu.make_async_remote_copy(
            src_ref=src,
            dst_ref=dst,
            send_sem=halo_send.at[which],
            recv_sem=halo_recv.at[which],
            device_id={"space": to},
            device_id_type=MESH,
        )

    pl.semaphore_wait(barrier, space_n - 1 + dp_n - 1)

    @pl.when(jnp.logical_not(last))
    def _():
        halo(0).start()

    @pl.when(jnp.logical_not(first))
    def _():
        halo(1).start()

    loads[0].wait()
    cotf[...] = cotb[...].reshape(512, LANES).astype(F32)
    for d in range(4):
        for hq in range(4):
            cots[pl.ds(d * 128 + hq * 32, 32), :] = cotf[
                pl.ds(d * 4 + hq, 32, stride=16), :
            ].astype(BF)

    for load in loads[1:]:
        load.wait()
    f1f[104:128, :] = jnp.zeros((24, 16), F32)
    for tap in range(27):
        f1f[tap * 4 : tap * 4 + 4, :] = f1b[tap].astype(F32)

    lane = iota((64, 512), 1)
    group = iota((64, 512), 0)
    spread = (
        (lane % 16 == group % 16) & (lane // 256 == group // 32) & ((lane // 64) % 2 == (group // 16) % 2)
    ).astype(F32).astype(BF)
    picked = dot(chosen[...], f1f[...].astype(BF)).astype(BF)
    rows = jnp.concatenate([picked[g * 192 : (g + 1) * 192] for g in range(4)], axis=1)
    rows = dot(rows, spread)
    lane8 = iota((8, 512), 1)
    reach = iota((8, 512), 0) - (2 * ((lane8 // 16) % 4) + (lane8 // 128) % 2) + 1
    near = [reach == kh for kh in range(3)]
    matrix = jnp.zeros((64, 8, 512), F32)
    for kh in range(3):
        piece = rows[kh * 64 : (kh + 1) * 64].reshape(64, 1, 512)
        matrix = jnp.where(near[kh][None], piece, matrix)
    w1[...] = matrix.reshape(512, 512).T.astype(BF)

    tile4 = (iota((32, 128), 0) == iota((32, 128), 1) % 32).astype(F32).astype(BF)
    wide = dot(f2b[...], tile4)
    group4 = iota((16, 128), 1) // 32
    parts = []
    for kd in range(3):
        for kw in range(3):
            for hq in range(4):
                block = jnp.zeros((16, 128), F32)
                for kh in range(3):
                    if 0 <= hq - kh + 1 < 4:
                        tap = (kd * 3 + kh) * 3 + kw
                        block = jnp.where(group4 == hq - kh + 1, wide[tap * 16 : tap * 16 + 16], block)
                parts.append(block)
    joined = jnp.concatenate(parts, axis=0)
    w2t[...] = joined.astype(BF)
    w2[...] = joined.T.astype(BF)

    bias_one = column(b1b[...], 16)
    bias_two = column(b2b[...], 32)
    take = iota((256, 512), 1)
    sample = (iota((256, 512), 0) == 2 * (take % 128) - 1 + take // 128).astype(F32).astype(BF)

    def split_columns(start, rows, to):
        source = raw[:, start : start + rows, :].reshape(4 * rows, 256)
        columns = dot(source, sample).reshape(4, rows, 512)[:, 8 : rows - 8]
        for s in range(4):
            shifted[s * 4 : s * 4 + 4, to : to + rows - 16] = columns[
                :, :, s * 128 : (s + 1) * 128
            ].astype(BF)

    lane64 = iota((64, 128), 1)

    def window(p):
        return shifted[:, p * 16 : p * 16 + 32, :].reshape(512, LANES)

    def layer_one(pair):
        both = dot(w1[...], jnp.concatenate([window(p) for p in pair], axis=1))
        for n, p in enumerate(pair):
            linear = both[:, n * 128 : (n + 1) * 128].reshape(32, 16, LANES) + bias_one[None]
            linear = linear.reshape(8, 64, LANES)
            slope = jnp.where(linear > 0, 1.0, 0.3)
            if 1 <= p <= 4:
                slopes[p - 1] = slope
            mean = jnp.sum(linear * slope, axis=0) * 0.125
            if p == 0:
                mean = jnp.where(first, 0.0, mean)
            if p == 5:
                mean = jnp.where(last, 0.0, mean)
            base = p * 192
            pooled[base : base + 64, :] = jnp.where(
                lane64 == 0, 0.0, pltpu.roll(mean, 1, axis=1)
            ).astype(BF)
            pooled[base + 64 : base + 128, :] = mean.astype(BF)
            pooled[base + 128 : base + 192, :] = jnp.where(
                lane64 == 127, 0.0, pltpu.roll(mean, 127, axis=1)
            ).astype(BF)

    def layer_two(pair):
        both = dot(
            w2[...],
            jnp.concatenate([pooled[j * 192 : j * 192 + 576, :] for j in pair], axis=1),
        )
        for n, j in enumerate(pair):
            linear = both[:, n * 128 : (n + 1) * 128].reshape(4, 32, LANES)
            linear = (linear + bias_two[None]).reshape(128, LANES)
            slope = jnp.where(linear > 0, 1.0, 0.3)
            errors_two[(j + 1) * 128 : (j + 2) * 128, :] = (
                cots[j * 128 : (j + 1) * 128, :].astype(F32) * slope
            ).astype(BF)
            out = linear * slope
            for hq in range(4):
                cotf[pl.ds(j * 4 + hq, 32, stride=16), :] = out[hq * 32 : (hq + 1) * 32]

    split_columns(RIM, 64, 32)
    layer_one((2, 3))

    @pl.when(jnp.logical_not(first))
    def _():
        halo(0).wait_recv()

    split_columns(0, 48, 0)

    @pl.when(jnp.logical_not(last))
    def _():
        halo(1).wait_recv()

    split_columns(80, 48, 80)
    layer_one((0, 5))
    layer_one((1, 4))
    layer_two((0, 3))

    @pl.when(jnp.logical_not(last))
    def _():
        halo(2).start()

    @pl.when(jnp.logical_not(first))
    def _():
        halo(3).start()

    layer_two((1, 2))
    act_here[...] = cotf[...].astype(BF).reshape(32, 16, LANES)
    act_store = pltpu.make_async_copy(act_here, act_out, out_sem.at[0])
    act_store.start()

    own = jnp.concatenate(
        [errors_two[j * 128 : (j + 1) * 128, :] for j in range(1, 5)], axis=1
    )
    near_in = jnp.concatenate(
        [pooled[j * 192 : j * 192 + 576, :] for j in range(4)], axis=1
    )
    near_in = jnp.concatenate([near_in, jnp.ones((16, 512), BF)], axis=0)
    outer = dot_nt(near_in, own)
    taps = []
    for kd in range(3):
        for kh in range(3):
            for kw in range(3):
                block = jnp.zeros((16, 128), F32)
                for hq in range(4):
                    if 0 <= hq - kh + 1 < 4:
                        at = ((kd * 3 + kw) * 4 + hq) * 16
                        block = jnp.where(group4 == hq - kh + 1, outer[at : at + 16], block)
                taps.append(fold(block, (64, 32)))
    taps.append(fold(outer[576:592], (64, 32)))
    for q in range(7):
        block = taps[4 * q]
        for slot in range(1, 4):
            block = jnp.where(group4 == slot, taps[4 * q + slot], block)
        terms[2 * q] = block[0:8]
        terms[2 * q + 1] = block[8:16]

    terms[14] = jnp.zeros((8, 128), F32)
    terms[15] = jnp.zeros((8, 128), F32)

    share = TILES // space_n

    def scatter(k):
        to = lax.rem(me + k, space_n)
        return pltpu.make_async_remote_copy(
            src_ref=terms.at[pl.ds(to * share, share)],
            dst_ref=landed.at[k - 1],
            send_sem=rs_send.at[k - 1],
            recv_sem=rs_recv.at[k - 1],
            device_id={"space": to},
            device_id_type=MESH,
        )

    def swap(axis, count, k, source, buffer, send, recv):
        return pltpu.make_async_remote_copy(
            src_ref=buffer.at[source],
            dst_ref=buffer.at[source],
            send_sem=send.at[k - 1],
            recv_sem=recv.at[k - 1],
            device_id={axis: lax.rem(lax.axis_index(axis) + k, count)},
            device_id_type=MESH,
        )

    def swap_start(axis, count, *where):
        for k in range(1, count):
            swap(axis, count, k, lax.axis_index(axis), *where).start()

    def swap_sent(axis, count, *where):
        for k in range(1, count):
            swap(axis, count, k, lax.axis_index(axis), *where).wait_send()

    def swap_landed(axis, count, *where):
        for k in range(1, count):
            source = lax.rem(lax.axis_index(axis) + count - k, count)
            swap(axis, count, k, source, *where).wait_recv()

    early_dp = ("dp", dp_n, across, dp_send, dp_recv)
    early_all = ("space", space_n, total, ag_send, ag_recv)
    last_space = ("space", space_n, late_space, ls_send, ls_recv)
    last_dp = ("dp", dp_n, late_dp, ld_send, ld_recv)

    back = jnp.concatenate([w2t[kd * 192 : (kd + 1) * 192, :] for kd in (2, 1, 0)], axis=1)

    def spread_back(pair):
        both = dot(
            back,
            jnp.concatenate([errors_two[q * 128 : q * 128 + 384, :] for q in pair], axis=1),
        )
        for n, q in enumerate(pair):
            three = both[:, n * 128 : (n + 1) * 128]
            grad = three[64:128]
            grad = grad + jnp.where(lane64 == 127, 0.0, pltpu.roll(three[0:64], 127, axis=1))
            grad = grad + jnp.where(lane64 == 0, 0.0, pltpu.roll(three[128:192], 1, axis=1))
            grad = grad.astype(BF).astype(F32)
            for hq in range(4):
                pgf[pl.ds(q * 4 + hq, 16, stride=16), :] = grad[hq * 16 : (hq + 1) * 16]
            errors_one[:, q * 128 : (q + 1) * 128] = (
                ((grad * 0.125)[None] * slopes[q]).astype(BF).reshape(512, LANES)
            )

    spread_back((1, 2))

    @pl.when(jnp.logical_not(first))
    def _():
        halo(2).wait_recv()

    @pl.when(jnp.logical_not(last))
    def _():
        halo(3).wait_recv()

    spread_back((0, 3))
    pg_here[...] = pgf[...].astype(BF).reshape(16, 16, LANES)
    pg_store = pltpu.make_async_copy(pg_here, pg_out, out_sem.at[1])
    pg_store.start()

    for k in range(1, space_n):
        scatter(k).start()

    near_in = jnp.concatenate([window(p) for p in range(1, 5)], axis=1)
    near_in = jnp.concatenate([near_in, jnp.ones((16, 512), BF)], axis=0)
    outer = dot_nt(near_in, errors_one[...])
    body = outer[0:512].reshape(4, 4, 4, 8, 512)
    low = iota((4, 3, 8, 128), 3) < 64
    for kh in range(3):
        summed = jnp.zeros((4, 4, 3, 8, 128), F32)
        for part in range(4):
            dd = part // 2
            cut = body[:, :, dd : dd + 3, :, part * 128 : (part + 1) * 128]
            mask = near[kh][:, part * 128 : (part + 1) * 128]
            summed = summed + jnp.where(mask[None, None, None], cut, 0.0)
        for kw in range(3):
            both = jnp.where(low, summed[kw], summed[kw + 1])
            for kd in range(3):
                tap = (kd * 3 + kh) * 3 + kw
                stack[tap * 32 : tap * 32 + 32, :] = both[:, kd].reshape(32, LANES)
    ones = outer[512:520]
    ones = ones[:, 0:128] + ones[:, 128:256] + ones[:, 256:384] + ones[:, 384:512]
    stack[864:872, :] = jnp.where(iota((8, 128), 0) == 0, ones, 0.0)
    stack[872:896, :] = jnp.zeros((24, 128), F32)
    gather = (iota((112, 896), 0) == iota((112, 896), 1) // 8).astype(F32).astype(BF)
    whole = stack[...]
    high = whole.astype(BF)
    rest = (whole - high.astype(F32)).astype(BF)
    reduced = fold(dot(gather, high) + dot(gather, rest), (64, 32, 16))
    group8 = iota((8, 128), 1) // 16
    for half in range(2):
        block = jnp.zeros((8, 128), F32)
        for slot in range(8):
            v = half * 8 + slot
            if v < 14:
                block = jnp.where(group8 == slot, reduced[v * 8 : v * 8 + 8], block)
        late[half] = block

    late_space[me] = late[...]
    swap_start(*last_space)

    sums = terms[pl.ds(me * share, share)]
    for k in range(1, space_n):
        scatter(k).wait_recv()
        sums = sums + landed[k - 1]
    across[mine] = sums
    swap_start(*early_dp)

    swap_landed(*last_space)
    sums = late_space[0]
    for k in range(1, space_n):
        sums = sums + late_space[k]
    late_dp[mine] = sums
    swap_start(*last_dp)

    swap_landed(*early_dp)
    sums = across[0]
    for k in range(1, dp_n):
        sums = sums + across[k]
    total[me] = sums
    swap_start(*early_all)

    swap_landed(*early_all)
    sums_here[0:TILES] = total[...].reshape(TILES, 8, 128)
    swap_landed(*last_dp)
    sums = late_dp[0]
    for k in range(1, dp_n):
        sums = sums + late_dp[k]
    sums_here[TILES : TILES + 2] = sums
    sums_store = pltpu.make_async_copy(sums_here, sums_out, out_sem.at[2])
    sums_store.start()

    for k in range(1, space_n):
        scatter(k).wait_send()
    swap_sent(*early_dp)
    swap_sent(*early_all)
    swap_sent(*last_space)
    swap_sent(*last_dp)
    act_store.wait()
    pg_store.wait()
    sums_store.wait()

    @pl.when(jnp.logical_not(last))
    def _():
        halo(0).wait_send()
        halo(2).wait_send()

    @pl.when(jnp.logical_not(first))
    def _():
        halo(1).wait_send()
        halo(3).wait_send()


def finish(scale_one, scale_two, act, pg, sums_in, act_out, pg_out, g1_out, s1_out, g2_out, s2_out,
           act_here, pg_here, sums_here, g1, s1, g2, s2, sem):
    load = pltpu.make_async_copy(sums_in, sums_here, sem.at[6])
    load.start()
    loads = [
        pltpu.make_async_copy(act, act_here, sem.at[7]),
        pltpu.make_async_copy(pg, pg_here, sem.at[8]),
    ]
    for copy in loads:
        copy.start()
    big = [
        pltpu.make_async_copy(act_here, act_out, sem.at[0]),
        pltpu.make_async_copy(pg_here, pg_out, sem.at[1]),
    ]
    for ready, copy in zip(loads, big):
        ready.wait()
        copy.start()
    load.wait()
    sums = sums_here[...]
    for q in range(7):
        block = jnp.concatenate([sums[2 * q], sums[2 * q + 1]], axis=0) * scale_two
        for slot in range(4):
            tap = 4 * q + slot
            turned = block if slot == 0 else pltpu.roll(block, 128 - 32 * slot, axis=1)
            if tap < 27:
                g2[tap * 16 : tap * 16 + 16, :] = turned[:, 0:32]
            else:
                s2[...] = turned[0:1, 0:32]
    for v in range(14):
        block = sums[TILES + v // 8] * scale_one
        slot = v % 8
        turned = block if slot == 0 else pltpu.roll(block, 128 - 16 * slot, axis=1)
        g1[2 * v] = turned[0:4, 0:16]
        if v < 13:
            g1[2 * v + 1] = turned[4:8, 0:16]
        else:
            s1[...] = turned[4:5, 0:16]
    small = [
        pltpu.make_async_copy(src, dst, sem.at[2 + n])
        for n, (src, dst) in enumerate(((g1, g1_out), (s1, s1_out), (g2, g2_out), (s2, s2_out)))
    ]
    for copy in small:
        copy.start()
    for copy in big + small:
        copy.wait()


def shards(dp_n, space_n, volume, first_filters, first_biases, second_filters, second_biases, cotangent):
    _, c_in, planes, high, wide = volume.shape
    c1, c2 = first_filters.shape[0], second_filters.shape[0]
    assert (c_in, planes, high, wide, c1, c2) == (4, 8, 8, 256, 16, 32)
    assert TILES % space_n == 0
    count_one = dp_n * space_n * planes * high * wide
    scale_one = 1.0 / math.sqrt(count_one)
    scale_two = 1.0 / math.sqrt(count_one / 8)
    share = TILES // space_n
    f1 = first_filters.transpose(2, 3, 4, 1, 0).reshape(27, 4, 16)
    f2 = second_filters.transpose(2, 3, 4, 1, 0).reshape(432, 32)
    vmem = pl.BlockSpec(memory_space=pltpu.VMEM)
    hbm = pl.BlockSpec(memory_space=pltpu.HBM)
    dma = pltpu.SemaphoreType.DMA
    act, pg, sums = pl.pallas_call(
        functools.partial(kernel, dp_n, space_n),
        out_shape=(
            jax.ShapeDtypeStruct((32, 16, 128), BF),
            jax.ShapeDtypeStruct((16, 16, 128), BF),
            jax.ShapeDtypeStruct((TILES + 2, 8, 128), F32),
        ),
        in_specs=[hbm] * 7,
        out_specs=(hbm,) * 3,
        scratch_shapes=[
            pltpu.VMEM((4, 2 * RIM + 64, 256), BF),
            pltpu.VMEM((32, 16, 128), BF),
            pltpu.VMEM((27, 4, 16), BF),
            pltpu.VMEM((128, 16), F32),
            pltpu.VMEM((432, 32), BF),
            pltpu.VMEM((1, 16), F32),
            pltpu.VMEM((1, 32), F32),
            pltpu.VMEM((768, 128), BF),
            pltpu.VMEM((512, 128), BF),
            pltpu.VMEM((512, 128), F32),
            pltpu.VMEM((16, 112, 128), BF),
            pltpu.VMEM((6 * 192, 128), BF),
            pltpu.VMEM((4, 8, 64, 128), F32),
            pltpu.VMEM((768, 128), BF),
            pltpu.VMEM((512, 512), BF),
            pltpu.VMEM((256, 128), F32),
            pltpu.VMEM((512, 512), BF),
            pltpu.VMEM((128, 576), BF),
            pltpu.VMEM((576, 128), BF),
            pltpu.VMEM((896, 128), F32),
            pltpu.VMEM((TILES, 8, 128), F32),
            pltpu.VMEM((space_n - 1, share, 8, 128), F32),
            pltpu.VMEM((dp_n, share, 8, 128), F32),
            pltpu.VMEM((space_n, share, 8, 128), F32),
            pltpu.VMEM((2, 8, 128), F32),
            pltpu.VMEM((space_n, 2, 8, 128), F32),
            pltpu.VMEM((dp_n, 2, 8, 128), F32),
            pltpu.VMEM((32, 16, 128), BF),
            pltpu.VMEM((16, 16, 128), BF),
            pltpu.VMEM((TILES + 2, 8, 128), F32),
            dma((3,)),
            dma((7,)),
            dma((4,)),
            dma((4,)),
        ]
        + [dma((space_n - 1,))] * 2
        + [dma((dp_n - 1,))] * 2
        + [dma((space_n - 1,))] * 4
        + [dma((dp_n - 1,))] * 2,
        compiler_params=pltpu.CompilerParams(
            collective_id=0, has_side_effects=True, vmem_limit_bytes=VMEM_LIMIT
        ),
    )(
        volume.reshape(4, 64, 256),
        cotangent.reshape(32, 16, 128),
        f1,
        f2,
        first_biases.reshape(1, 16),
        second_biases.reshape(1, 32),
        jnp.asarray(tap_choice(), BF),
    )
    act, pg, g1, s1, g2, s2 = pl.pallas_call(
        functools.partial(finish, scale_one, scale_two),
        out_shape=(
            jax.ShapeDtypeStruct((32, 16, 128), BF),
            jax.ShapeDtypeStruct((16, 16, 128), BF),
            jax.ShapeDtypeStruct((27, 4, 16), F32),
            jax.ShapeDtypeStruct((1, 16), F32),
            jax.ShapeDtypeStruct((432, 32), F32),
            jax.ShapeDtypeStruct((1, 32), F32),
        ),
        in_specs=[hbm] * 3,
        out_specs=(hbm,) * 6,
        scratch_shapes=[
            pltpu.VMEM((32, 16, 128), BF),
            pltpu.VMEM((16, 16, 128), BF),
            pltpu.VMEM((TILES + 2, 8, 128), F32),
            pltpu.VMEM((27, 4, 16), F32),
            pltpu.VMEM((1, 16), F32),
            pltpu.VMEM((432, 32), F32),
            pltpu.VMEM((1, 32), F32),
            dma((9,)),
        ],
        compiler_params=pltpu.CompilerParams(vmem_limit_bytes=VMEM_LIMIT),
    )(act, pg, sums)
    return (
        act.reshape(1, 32, 4, 4, 128),
        pg.reshape(1, 16, 4, 4, 128),
        g1.reshape(3, 3, 3, 4, 16).transpose(4, 3, 0, 1, 2),
        s1.reshape(16),
        g2.reshape(3, 3, 3, 16, 32).transpose(4, 3, 0, 1, 2),
        s2.reshape(32),
    )


def solution(mesh):
    placed = (
        P("dp", None, "space", None, None),
        P(),
        P(),
        P(),
        P(),
        P("dp", None, "space", None, None),
    )
    return jax.shard_map(
        functools.partial(shards, mesh.shape["dp"], mesh.shape["space"]),
        mesh=mesh,
        in_specs=placed,
        out_specs=(
            P("dp", None, "space", None, None),
            P("dp", None, "space", None, None),
            P(),
            P(),
            P(),
            P(),
        ),
        check_vma=False,
    )
```

```python
import functools
import math

import jax
import jax.numpy as jnp
import numpy as np
from jax import lax
from jax.experimental import pallas as pl
from jax.experimental.pallas import tpu as pltpu
from jax.sharding import PartitionSpec as P

BF = jnp.bfloat16
F32 = jnp.float32
MESH = pl.DeviceIdType.MESH
LANES = 128
RIM = 48
VMEM_LIMIT = 60 * 1024 * 1024
TILES = 16


def tap_choice():
    table = np.zeros((2, 2, 3, 4, 4, 4, 128), np.float32)
    for dd in range(2):
        for wpar in range(2):
            for kh in range(3):
                for s in range(4):
                    for dz in range(4):
                        kd, kw = dz - dd, s - wpar
                        if 0 <= kd < 3 and 0 <= kw < 3:
                            for i in range(4):
                                table[dd, wpar, kh, s, i, dz, ((kd * 3 + kh) * 3 + kw) * 4 + i] = 1
    return table.reshape(4 * 192, 128)


def iota(shape, dim):
    return lax.broadcasted_iota(jnp.int32, shape, dim)


def dot(a, b):
    return jnp.dot(a, b, preferred_element_type=F32)


def dot_nt(a, b):
    return lax.dot_general(a, b, (((1,), (1,)), ((), ())), preferred_element_type=F32)


def column(row, count):
    return jnp.sum(
        jnp.where(iota((count, count), 0) == iota((count, count), 1), row, 0.0),
        axis=1,
        keepdims=True,
    )


def fold(values, steps):
    for step in steps:
        values = values + pltpu.roll(values, step, axis=values.ndim - 1)
    return values


def kernel(
    dp_n, space_n,
    vol, cot, f1, f2, b1, b2, choice,
    act_out, pg_out, sums_out,
    raw, cotb, f1b, f1f, f2b, b1b, b2b, chosen,
    cots, cotf, shifted, pooled, slopes, errors_two, errors_one, pgf, w1, w2, w2t,
    stack, terms, landed, across, total, late, late_space, late_dp,
    act_here, pg_here, sums_here, out_sem, in_sem, halo_send, halo_recv, rs_send, rs_recv, dp_send, dp_recv, ag_send, ag_recv,
    ls_send, ls_recv, ld_send, ld_recv,
):
    me = lax.axis_index("space")
    mine = lax.axis_index("dp")
    first = me == 0
    last = me == space_n - 1

    barrier = pltpu.get_barrier_semaphore()
    for k in range(1, space_n):
        pl.semaphore_signal(
            barrier, inc=1, device_id={"space": lax.rem(me + k, space_n)}, device_id_type=MESH
        )
    for k in range(1, dp_n):
        pl.semaphore_signal(
            barrier, inc=1, device_id={"dp": lax.rem(mine + k, dp_n)}, device_id_type=MESH
        )
    loads = [
        pltpu.make_async_copy(src, dst, in_sem.at[n])
        for n, (src, dst) in enumerate(
            (
                (cot, cotb),
                (f1, f1b),
                (choice, chosen),
                (f2, f2b),
                (b1, b1b),
                (b2, b2b),
                (vol, raw.at[:, RIM : RIM + 64]),
            )
        )
    ]
    for load in loads:
        load.start()

    @pl.when(first)
    def _():
        raw[:, 0:RIM, :] = jnp.zeros((4, RIM, 256), BF)
        cots[0:128, :] = jnp.zeros((128, LANES), BF)

    @pl.when(last)
    def _():
        raw[:, RIM + 64 :, :] = jnp.zeros((4, RIM, 256), BF)
        cots[640:768, :] = jnp.zeros((128, LANES), BF)

    right = lax.rem(me + 1, space_n)
    left = lax.rem(me + space_n - 1, space_n)

    def halo(which):
        src, dst, to = (
            (vol.at[:, 16:64], raw.at[:, 0:RIM], right),
            (vol.at[:, 0:RIM], raw.at[:, RIM + 64 : 2 * RIM + 64], left),
            (cots.at[512:640], cots.at[0:128], right),
            (cots.at[128:256], cots.at[640:768], left),
        )[which]
        return pltpu.make_async_remote_copy(
            src_ref=src,
            dst_ref=dst,
            send_sem=halo_send.at[which],
            recv_sem=halo_recv.at[which],
            device_id={"space": to},
            device_id_type=MESH,
        )

    pl.semaphore_wait(barrier, space_n - 1 + dp_n - 1)

    @pl.when(jnp.logical_not(last))
    def _():
        halo(0).start()

    @pl.when(jnp.logical_not(first))
    def _():
        halo(1).start()

    loads[0].wait()
    cotf[...] = cotb[...].reshape(512, LANES).astype(F32)
    for d in range(4):
        for hq in range(4):
            cots[pl.ds((1 + d) * 128 + hq * 32, 32), :] = cotf[
                pl.ds(d * 4 + hq, 32, stride=16), :
            ].astype(BF)

    @pl.when(jnp.logical_not(last))
    def _():
        halo(2).start()

    @pl.when(jnp.logical_not(first))
    def _():
        halo(3).start()

    for load in loads[1:]:
        load.wait()
    f1f[...] = jnp.zeros((128, 128), F32)
    for tap in range(27):
        f1f[tap * 4 : tap * 4 + 4, 0:16] = f1b[tap].astype(F32)

    picked = dot_nt(f1f[...].T[0:16].astype(BF), chosen[...])
    picked = jnp.concatenate([picked[:, g * 64 : (g + 1) * 64] for g in range(12)], axis=0)
    repeat = (iota((64, 512), 0) == iota((64, 512), 1) // 8).astype(F32).astype(BF)
    rows = dot(picked.astype(BF), repeat)
    height = iota((16, 512), 1) % 8
    for dd in range(2):
        for hpar in range(2):
            for wpar in range(2):
                for hq in range(4):
                    block = jnp.zeros((16, 512), F32)
                    for kh in range(3):
                        at = ((dd * 2 + wpar) * 3 + kh) * 16
                        block = jnp.where(
                            height == 2 * hq + hpar + kh - 1, rows[at : at + 16], block
                        )
                    at = (((dd * 2 + hpar) * 2 + wpar) * 4 + hq) * 16
                    w1[at : at + 16, :] = block.astype(BF)
    lane8 = iota((8, 512), 1)
    reach = iota((8, 512), 0) - (2 * ((lane8 // 16) % 4) + (lane8 // 128) % 2) + 1
    near = [reach == kh for kh in range(3)]
    tile4 = (iota((32, 128), 0) == iota((32, 128), 1) % 32).astype(F32).astype(BF)
    wide = dot(f2b[...], tile4)
    group4 = iota((16, 128), 1) // 32
    parts = []
    for kd in range(3):
        for kw in range(3):
            for hq in range(4):
                block = jnp.zeros((16, 128), F32)
                for kh in range(3):
                    if 0 <= hq - kh + 1 < 4:
                        tap = (kd * 3 + kh) * 3 + kw
                        block = jnp.where(group4 == hq - kh + 1, wide[tap * 16 : tap * 16 + 16], block)
                parts.append(block)
    joined = jnp.concatenate(parts, axis=0)
    w2t[...] = joined.astype(BF)
    w2[...] = joined.T.astype(BF)

    bias_one = column(b1b[...], 16)
    bias_two = column(b2b[...], 32)
    take = iota((256, 512), 1)
    sample = (iota((256, 512), 0) == 2 * (take % 128) - 1 + take // 128).astype(F32).astype(BF)

    def split_columns(part):
        source = raw[:, part * RIM : part * RIM + 64, :].reshape(256, 256)
        columns = dot(source, sample).reshape(4, 64, 512)[:, 8:56]
        for s in range(4):
            shifted[s * 4 : s * 4 + 4, part * RIM : part * RIM + RIM] = columns[
                :, :, s * 128 : (s + 1) * 128
            ].astype(BF)

    lane64 = iota((64, 128), 1)

    def window(p):
        return shifted[:, p * 16 : p * 16 + 32, :].reshape(512, LANES)

    def layer_one(pair):
        both = dot(w1[...], jnp.concatenate([window(p) for p in pair], axis=1))
        for n, p in enumerate(pair):
            linear = both[:, n * 128 : (n + 1) * 128].reshape(32, 16, LANES) + bias_one[None]
            linear = linear.reshape(8, 64, LANES)
            slope = jnp.where(linear > 0, 1.0, 0.3)
            if 2 <= p <= 5:
                slopes[p - 2] = slope
            mean = jnp.sum(linear * slope, axis=0) * 0.125
            if p < 2:
                mean = jnp.where(first, 0.0, mean)
            if p > 5:
                mean = jnp.where(last, 0.0, mean)
            base = p * 192
            pooled[base : base + 64, :] = jnp.where(
                lane64 == 0, 0.0, pltpu.roll(mean, 1, axis=1)
            ).astype(BF)
            pooled[base + 64 : base + 128, :] = mean.astype(BF)
            pooled[base + 128 : base + 192, :] = jnp.where(
                lane64 == 127, 0.0, pltpu.roll(mean, 127, axis=1)
            ).astype(BF)

    def layer_two(pair):
        both = dot(
            w2[...],
            jnp.concatenate([pooled[j * 192 : j * 192 + 576, :] for j in pair], axis=1),
        )
        for n, j in enumerate(pair):
            linear = both[:, n * 128 : (n + 1) * 128].reshape(4, 32, LANES)
            linear = (linear + bias_two[None]).reshape(128, LANES)
            slope = jnp.where(linear > 0, 1.0, 0.3)
            errors_two[j * 128 : (j + 1) * 128, :] = (
                cots[j * 128 : (j + 1) * 128, :].astype(F32) * slope
            ).astype(BF)
            if 1 <= j <= 4:
                out = linear * slope
                for hq in range(4):
                    cotf[pl.ds((j - 1) * 4 + hq, 32, stride=16), :] = out[hq * 32 : (hq + 1) * 32]

    split_columns(1)
    layer_one((3, 4))

    @pl.when(jnp.logical_not(first))
    def _():
        halo(0).wait_recv()

    split_columns(0)

    @pl.when(jnp.logical_not(last))
    def _():
        halo(1).wait_recv()

    split_columns(2)
    layer_one((2, 5))
    layer_one((1, 6))
    layer_one((0, 7))
    layer_two((2, 3))
    layer_two((1, 4))

    @pl.when(jnp.logical_not(first))
    def _():
        halo(2).wait_recv()

    @pl.when(jnp.logical_not(last))
    def _():
        halo(3).wait_recv()

    layer_two((0, 5))
    act_here[...] = cotf[...].astype(BF).reshape(32, 16, LANES)
    act_store = pltpu.make_async_copy(act_here, act_out, out_sem.at[0])
    act_store.start()

    own = jnp.concatenate(
        [errors_two[j * 128 : (j + 1) * 128, :] for j in range(1, 5)], axis=1
    )
    near_in = jnp.concatenate(
        [pooled[j * 192 : j * 192 + 576, :] for j in range(1, 5)], axis=1
    )
    near_in = jnp.concatenate([near_in, jnp.ones((16, 512), BF)], axis=0)
    outer = dot_nt(near_in, own)
    taps = []
    for kd in range(3):
        for kh in range(3):
            for kw in range(3):
                block = jnp.zeros((16, 128), F32)
                for hq in range(4):
                    if 0 <= hq - kh + 1 < 4:
                        at = ((kd * 3 + kw) * 4 + hq) * 16
                        block = jnp.where(group4 == hq - kh + 1, outer[at : at + 16], block)
                taps.append(fold(block, (64, 32)))
    taps.append(fold(outer[576:592], (64, 32)))
    for q in range(7):
        block = taps[4 * q]
        for slot in range(1, 4):
            block = jnp.where(group4 == slot, taps[4 * q + slot], block)
        terms[2 * q] = block[0:8]
        terms[2 * q + 1] = block[8:16]

    terms[14] = jnp.zeros((8, 128), F32)
    terms[15] = jnp.zeros((8, 128), F32)

    share = TILES // space_n

    def scatter(k):
        to = lax.rem(me + k, space_n)
        return pltpu.make_async_remote_copy(
            src_ref=terms.at[pl.ds(to * share, share)],
            dst_ref=landed.at[k - 1],
            send_sem=rs_send.at[k - 1],
            recv_sem=rs_recv.at[k - 1],
            device_id={"space": to},
            device_id_type=MESH,
        )

    def swap(axis, count, k, source, buffer, send, recv):
        return pltpu.make_async_remote_copy(
            src_ref=buffer.at[source],
            dst_ref=buffer.at[source],
            send_sem=send.at[k - 1],
            recv_sem=recv.at[k - 1],
            device_id={axis: lax.rem(lax.axis_index(axis) + k, count)},
            device_id_type=MESH,
        )

    def swap_start(axis, count, *where):
        for k in range(1, count):
            swap(axis, count, k, lax.axis_index(axis), *where).start()

    def swap_sent(axis, count, *where):
        for k in range(1, count):
            swap(axis, count, k, lax.axis_index(axis), *where).wait_send()

    def swap_landed(axis, count, *where):
        for k in range(1, count):
            source = lax.rem(lax.axis_index(axis) + count - k, count)
            swap(axis, count, k, source, *where).wait_recv()

    early_dp = ("dp", dp_n, across, dp_send, dp_recv)
    early_all = ("space", space_n, total, ag_send, ag_recv)
    last_space = ("space", space_n, late_space, ls_send, ls_recv)
    last_dp = ("dp", dp_n, late_dp, ld_send, ld_recv)

    for k in range(1, space_n):
        scatter(k).start()

    back = jnp.concatenate([w2t[kd * 192 : (kd + 1) * 192, :] for kd in (2, 1, 0)], axis=1)
    quad = dot(
        back,
        jnp.concatenate([errors_two[q * 128 : q * 128 + 384, :] for q in range(4)], axis=1),
    )
    for q in range(4):
        three = quad[:, q * 128 : (q + 1) * 128]
        grad = three[64:128]
        grad = grad + jnp.where(lane64 == 127, 0.0, pltpu.roll(three[0:64], 127, axis=1))
        grad = grad + jnp.where(lane64 == 0, 0.0, pltpu.roll(three[128:192], 1, axis=1))
        grad = grad.astype(BF).astype(F32)
        for hq in range(4):
            pgf[pl.ds(q * 4 + hq, 16, stride=16), :] = grad[hq * 16 : (hq + 1) * 16]
        errors_one[:, q * 128 : (q + 1) * 128] = (
            ((grad * 0.125)[None] * slopes[q]).astype(BF).reshape(512, LANES)
        )
    pg_here[...] = pgf[...].astype(BF).reshape(16, 16, LANES)
    pg_store = pltpu.make_async_copy(pg_here, pg_out, out_sem.at[1])
    pg_store.start()

    near_in = jnp.concatenate([window(p) for p in range(2, 6)], axis=1)
    near_in = jnp.concatenate([near_in, jnp.ones((16, 512), BF)], axis=0)
    outer = dot_nt(near_in, errors_one[...])
    body = outer[0:512].reshape(4, 4, 4, 8, 512)
    low = iota((4, 3, 8, 128), 3) < 64
    for kh in range(3):
        summed = jnp.zeros((4, 4, 3, 8, 128), F32)
        for part in range(4):
            dd = part // 2
            cut = body[:, :, dd : dd + 3, :, part * 128 : (part + 1) * 128]
            mask = near[kh][:, part * 128 : (part + 1) * 128]
            summed = summed + jnp.where(mask[None, None, None], cut, 0.0)
        for kw in range(3):
            both = jnp.where(low, summed[kw], summed[kw + 1])
            for kd in range(3):
                tap = (kd * 3 + kh) * 3 + kw
                stack[tap * 32 : tap * 32 + 32, :] = both[:, kd].reshape(32, LANES)
    ones = outer[512:520]
    ones = ones[:, 0:128] + ones[:, 128:256] + ones[:, 256:384] + ones[:, 384:512]
    stack[864:872, :] = jnp.where(iota((8, 128), 0) == 0, ones, 0.0)
    stack[872:896, :] = jnp.zeros((24, 128), F32)
    sums = terms[pl.ds(me * share, share)]
    for k in range(1, space_n):
        scatter(k).wait_recv()
        sums = sums + landed[k - 1]
    across[mine] = sums
    swap_start(*early_dp)

    gather = (iota((112, 896), 0) == iota((112, 896), 1) // 8).astype(F32).astype(BF)
    whole = stack[...]
    high = whole.astype(BF)
    rest = (whole - high.astype(F32)).astype(BF)
    reduced = fold(dot(gather, high) + dot(gather, rest), (64, 32, 16))
    group8 = iota((8, 128), 1) // 16
    for half in range(2):
        block = jnp.zeros((8, 128), F32)
        for slot in range(8):
            v = half * 8 + slot
            if v < 14:
                block = jnp.where(group8 == slot, reduced[v * 8 : v * 8 + 8], block)
        late[half] = block

    late_space[me] = late[...]
    swap_start(*last_space)

    swap_landed(*early_dp)
    sums = across[0]
    for k in range(1, dp_n):
        sums = sums + across[k]
    total[me] = sums
    swap_start(*early_all)

    swap_landed(*last_space)
    sums = late_space[0]
    for k in range(1, space_n):
        sums = sums + late_space[k]
    late_dp[mine] = sums
    swap_start(*last_dp)

    swap_landed(*early_all)
    sums_here[0:TILES] = total[...].reshape(TILES, 8, 128)
    swap_landed(*last_dp)
    sums = late_dp[0]
    for k in range(1, dp_n):
        sums = sums + late_dp[k]
    sums_here[TILES : TILES + 2] = sums
    sums_store = pltpu.make_async_copy(sums_here, sums_out, out_sem.at[2])
    sums_store.start()

    for k in range(1, space_n):
        scatter(k).wait_send()
    swap_sent(*early_dp)
    swap_sent(*early_all)
    swap_sent(*last_space)
    swap_sent(*last_dp)
    act_store.wait()
    pg_store.wait()
    sums_store.wait()

    @pl.when(jnp.logical_not(last))
    def _():
        halo(0).wait_send()
        halo(2).wait_send()

    @pl.when(jnp.logical_not(first))
    def _():
        halo(1).wait_send()
        halo(3).wait_send()


def finish(scale_one, scale_two, act, pg, sums_in, act_out, pg_out, g1_out, s1_out, g2_out, s2_out,
           act_here, pg_here, sums_here, g1, s1, g2, s2, sem):
    load = pltpu.make_async_copy(sums_in, sums_here, sem.at[6])
    load.start()
    loads = [
        pltpu.make_async_copy(act, act_here, sem.at[7]),
        pltpu.make_async_copy(pg, pg_here, sem.at[8]),
    ]
    for copy in loads:
        copy.start()
    big = [
        pltpu.make_async_copy(act_here, act_out, sem.at[0]),
        pltpu.make_async_copy(pg_here, pg_out, sem.at[1]),
    ]
    for ready, copy in zip(loads, big):
        ready.wait()
        copy.start()
    load.wait()
    sums = sums_here[...]
    for q in range(7):
        block = jnp.concatenate([sums[2 * q], sums[2 * q + 1]], axis=0) * scale_two
        for slot in range(4):
            tap = 4 * q + slot
            turned = block if slot == 0 else pltpu.roll(block, 128 - 32 * slot, axis=1)
            if tap < 27:
                g2[tap * 16 : tap * 16 + 16, :] = turned[:, 0:32]
            else:
                s2[...] = turned[0:1, 0:32]
    for v in range(14):
        block = sums[TILES + v // 8] * scale_one
        slot = v % 8
        turned = block if slot == 0 else pltpu.roll(block, 128 - 16 * slot, axis=1)
        g1[2 * v] = turned[0:4, 0:16]
        if v < 13:
            g1[2 * v + 1] = turned[4:8, 0:16]
        else:
            s1[...] = turned[4:5, 0:16]
    small = [
        pltpu.make_async_copy(src, dst, sem.at[2 + n])
        for n, (src, dst) in enumerate(((g1, g1_out), (s1, s1_out), (g2, g2_out), (s2, s2_out)))
    ]
    for copy in small:
        copy.start()
    for copy in big + small:
        copy.wait()


def shards(dp_n, space_n, volume, first_filters, first_biases, second_filters, second_biases, cotangent):
    _, c_in, planes, high, wide = volume.shape
    c1, c2 = first_filters.shape[0], second_filters.shape[0]
    assert (c_in, planes, high, wide, c1, c2) == (4, 8, 8, 256, 16, 32)
    assert TILES % space_n == 0
    count_one = dp_n * space_n * planes * high * wide
    scale_one = 1.0 / math.sqrt(count_one)
    scale_two = 1.0 / math.sqrt(count_one / 8)
    share = TILES // space_n
    f1 = first_filters.transpose(2, 3, 4, 1, 0).reshape(27, 4, 16)
    f2 = second_filters.transpose(2, 3, 4, 1, 0).reshape(432, 32)
    vmem = pl.BlockSpec(memory_space=pltpu.VMEM)
    hbm = pl.BlockSpec(memory_space=pltpu.HBM)
    dma = pltpu.SemaphoreType.DMA
    act, pg, sums = pl.pallas_call(
        functools.partial(kernel, dp_n, space_n),
        out_shape=(
            jax.ShapeDtypeStruct((32, 16, 128), BF),
            jax.ShapeDtypeStruct((16, 16, 128), BF),
            jax.ShapeDtypeStruct((TILES + 2, 8, 128), F32),
        ),
        in_specs=[hbm] * 7,
        out_specs=(hbm,) * 3,
        scratch_shapes=[
            pltpu.VMEM((4, 2 * RIM + 64, 256), BF),
            pltpu.VMEM((32, 16, 128), BF),
            pltpu.VMEM((27, 4, 16), BF),
            pltpu.VMEM((128, 128), F32),
            pltpu.VMEM((432, 32), BF),
            pltpu.VMEM((1, 16), F32),
            pltpu.VMEM((1, 32), F32),
            pltpu.VMEM((768, 128), BF),
            pltpu.VMEM((768, 128), BF),
            pltpu.VMEM((512, 128), F32),
            pltpu.VMEM((16, 144, 128), BF),
            pltpu.VMEM((8 * 192, 128), BF),
            pltpu.VMEM((4, 8, 64, 128), F32),
            pltpu.VMEM((768, 128), BF),
            pltpu.VMEM((512, 512), BF),
            pltpu.VMEM((256, 128), F32),
            pltpu.VMEM((512, 512), BF),
            pltpu.VMEM((128, 576), BF),
            pltpu.VMEM((576, 128), BF),
            pltpu.VMEM((896, 128), F32),
            pltpu.VMEM((TILES, 8, 128), F32),
            pltpu.VMEM((space_n - 1, share, 8, 128), F32),
            pltpu.VMEM((dp_n, share, 8, 128), F32),
            pltpu.VMEM((space_n, share, 8, 128), F32),
            pltpu.VMEM((2, 8, 128), F32),
            pltpu.VMEM((space_n, 2, 8, 128), F32),
            pltpu.VMEM((dp_n, 2, 8, 128), F32),
            pltpu.VMEM((32, 16, 128), BF),
            pltpu.VMEM((16, 16, 128), BF),
            pltpu.VMEM((TILES + 2, 8, 128), F32),
            dma((3,)),
            dma((7,)),
            dma((4,)),
            dma((4,)),
        ]
        + [dma((space_n - 1,))] * 2
        + [dma((dp_n - 1,))] * 2
        + [dma((space_n - 1,))] * 4
        + [dma((dp_n - 1,))] * 2,
        compiler_params=pltpu.CompilerParams(
            collective_id=0, has_side_effects=True, vmem_limit_bytes=VMEM_LIMIT
        ),
    )(
        volume.reshape(4, 64, 256),
        cotangent.reshape(32, 16, 128),
        f1,
        f2,
        first_biases.reshape(1, 16),
        second_biases.reshape(1, 32),
        jnp.asarray(tap_choice(), BF),
    )
    act, pg, g1, s1, g2, s2 = pl.pallas_call(
        functools.partial(finish, scale_one, scale_two),
        out_shape=(
            jax.ShapeDtypeStruct((32, 16, 128), BF),
            jax.ShapeDtypeStruct((16, 16, 128), BF),
            jax.ShapeDtypeStruct((27, 4, 16), F32),
            jax.ShapeDtypeStruct((1, 16), F32),
            jax.ShapeDtypeStruct((432, 32), F32),
            jax.ShapeDtypeStruct((1, 32), F32),
        ),
        in_specs=[hbm] * 3,
        out_specs=(hbm,) * 6,
        scratch_shapes=[
            pltpu.VMEM((32, 16, 128), BF),
            pltpu.VMEM((16, 16, 128), BF),
            pltpu.VMEM((TILES + 2, 8, 128), F32),
            pltpu.VMEM((27, 4, 16), F32),
            pltpu.VMEM((1, 16), F32),
            pltpu.VMEM((432, 32), F32),
            pltpu.VMEM((1, 32), F32),
            dma((9,)),
        ],
        compiler_params=pltpu.CompilerParams(vmem_limit_bytes=VMEM_LIMIT),
    )(act, pg, sums)
    return (
        act.reshape(1, 32, 4, 4, 128),
        pg.reshape(1, 16, 4, 4, 128),
        g1.reshape(3, 3, 3, 4, 16).transpose(4, 3, 0, 1, 2),
        s1.reshape(16),
        g2.reshape(3, 3, 3, 16, 32).transpose(4, 3, 0, 1, 2),
        s2.reshape(32),
    )


def solution(mesh):
    placed = (
        P("dp", None, "space", None, None),
        P(),
        P(),
        P(),
        P(),
        P("dp", None, "space", None, None),
    )
    return jax.shard_map(
        functools.partial(shards, mesh.shape["dp"], mesh.shape["space"]),
        mesh=mesh,
        in_specs=placed,
        out_specs=(
            P("dp", None, "space", None, None),
            P("dp", None, "space", None, None),
            P(),
            P(),
            P(),
            P(),
        ),
        check_vma=False,
    )
```

```python
import functools
import math

import jax
import jax.numpy as jnp
import numpy as np
from jax import lax
from jax.experimental import pallas as pl
from jax.experimental.pallas import tpu as pltpu
from jax.sharding import PartitionSpec as P

BF = jnp.bfloat16
F32 = jnp.float32
MESH = pl.DeviceIdType.MESH
LANES = 128
RIM = 48
VMEM_LIMIT = 60 * 1024 * 1024
TILES = 16


def tap_choice():
    table = np.zeros((2, 2, 3, 4, 4, 4, 128), np.float32)
    for dd in range(2):
        for wpar in range(2):
            for kh in range(3):
                for s in range(4):
                    for dz in range(4):
                        kd, kw = dz - dd, s - wpar
                        if 0 <= kd < 3 and 0 <= kw < 3:
                            for i in range(4):
                                table[dd, wpar, kh, s, i, dz, ((kd * 3 + kh) * 3 + kw) * 4 + i] = 1
    return table.reshape(4 * 192, 128)


def iota(shape, dim):
    return lax.broadcasted_iota(jnp.int32, shape, dim)


def dot(a, b):
    return jnp.dot(a, b, preferred_element_type=F32)


def dot_nt(a, b):
    return lax.dot_general(a, b, (((1,), (1,)), ((), ())), preferred_element_type=F32)


def column(row, count):
    return jnp.sum(
        jnp.where(iota((count, count), 0) == iota((count, count), 1), row, 0.0),
        axis=1,
        keepdims=True,
    )


def fold(values, steps):
    for step in steps:
        values = values + pltpu.roll(values, step, axis=values.ndim - 1)
    return values


def kernel(
    dp_n, space_n,
    vol, cot, f1, f2, b1, b2, choice,
    act_out, pg_out, sums_out,
    raw, cotb, f1b, f1f, f2b, b1b, b2b, chosen,
    cots, cotf, shifted, pooled, slopes, errors_two, errors_one, pgf, w1, w2, w2t,
    stack, terms, landed, across, total, late, late_space, late_dp,
    act_here, pg_here, sums_here, out_sem, in_sem, halo_send, halo_recv, rs_send, rs_recv, dp_send, dp_recv, ag_send, ag_recv,
    ls_send, ls_recv, ld_send, ld_recv,
):
    me = lax.axis_index("space")
    mine = lax.axis_index("dp")
    first = me == 0
    last = me == space_n - 1

    barrier = pltpu.get_barrier_semaphore()
    for k in range(1, space_n):
        pl.semaphore_signal(
            barrier, inc=1, device_id={"space": lax.rem(me + k, space_n)}, device_id_type=MESH
        )
    for k in range(1, dp_n):
        pl.semaphore_signal(
            barrier, inc=1, device_id={"dp": lax.rem(mine + k, dp_n)}, device_id_type=MESH
        )
    loads = [
        pltpu.make_async_copy(src, dst, in_sem.at[n])
        for n, (src, dst) in enumerate(
            (
                (cot, cotb),
                (f1, f1b),
                (choice, chosen),
                (f2, f2b),
                (b1, b1b),
                (b2, b2b),
                (vol, raw.at[:, RIM : RIM + 64]),
            )
        )
    ]
    for load in loads:
        load.start()

    @pl.when(first)
    def _():
        raw[:, 0:RIM, :] = jnp.zeros((4, RIM, 256), BF)
        cots[0:128, :] = jnp.zeros((128, LANES), BF)

    @pl.when(last)
    def _():
        raw[:, RIM + 64 :, :] = jnp.zeros((4, RIM, 256), BF)
        cots[640:768, :] = jnp.zeros((128, LANES), BF)

    right = lax.rem(me + 1, space_n)
    left = lax.rem(me + space_n - 1, space_n)

    def halo(which):
        src, dst, to = (
            (vol.at[:, 16:64], raw.at[:, 0:RIM], right),
            (vol.at[:, 0:RIM], raw.at[:, RIM + 64 : 2 * RIM + 64], left),
            (cots.at[512:640], cots.at[0:128], right),
            (cots.at[128:256], cots.at[640:768], left),
        )[which]
        return pltpu.make_async_remote_copy(
            src_ref=src,
            dst_ref=dst,
            send_sem=halo_send.at[which],
            recv_sem=halo_recv.at[which],
            device_id={"space": to},
            device_id_type=MESH,
        )

    pl.semaphore_wait(barrier, space_n - 1 + dp_n - 1)

    @pl.when(jnp.logical_not(last))
    def _():
        halo(0).start()

    @pl.when(jnp.logical_not(first))
    def _():
        halo(1).start()

    loads[0].wait()
    cotf[...] = cotb[...].reshape(512, LANES).astype(F32)
    for d in range(4):
        for hq in range(4):
            cots[pl.ds((1 + d) * 128 + hq * 32, 32), :] = cotf[
                pl.ds(d * 4 + hq, 32, stride=16), :
            ].astype(BF)

    @pl.when(jnp.logical_not(last))
    def _():
        halo(2).start()

    @pl.when(jnp.logical_not(first))
    def _():
        halo(3).start()

    for load in loads[1:]:
        load.wait()
    f1f[...] = jnp.zeros((128, 128), F32)
    for tap in range(27):
        f1f[tap * 4 : tap * 4 + 4, 0:16] = f1b[tap].astype(F32)

    picked = dot_nt(f1f[...].T[0:16].astype(BF), chosen[...])
    picked = jnp.concatenate([picked[:, g * 64 : (g + 1) * 64] for g in range(12)], axis=0)
    repeat = (iota((64, 512), 0) == iota((64, 512), 1) // 8).astype(F32).astype(BF)
    rows = dot(picked.astype(BF), repeat)
    height = iota((16, 512), 1) % 8
    for dd in range(2):
        for hpar in range(2):
            for wpar in range(2):
                for hq in range(4):
                    block = jnp.zeros((16, 512), F32)
                    for kh in range(3):
                        at = ((dd * 2 + wpar) * 3 + kh) * 16
                        block = jnp.where(
                            height == 2 * hq + hpar + kh - 1, rows[at : at + 16], block
                        )
                    at = (((dd * 2 + hpar) * 2 + wpar) * 4 + hq) * 16
                    w1[at : at + 16, :] = block.astype(BF)
    lane8 = iota((8, 512), 1)
    reach = iota((8, 512), 0) - (2 * ((lane8 // 16) % 4) + (lane8 // 128) % 2) + 1
    near = [reach == kh for kh in range(3)]
    tile4 = (iota((32, 128), 0) == iota((32, 128), 1) % 32).astype(F32).astype(BF)
    wide = dot(f2b[...], tile4)
    group4 = iota((16, 128), 1) // 32
    parts = []
    for kd in range(3):
        for kw in range(3):
            for hq in range(4):
                block = jnp.zeros((16, 128), F32)
                for kh in range(3):
                    if 0 <= hq - kh + 1 < 4:
                        tap = (kd * 3 + kh) * 3 + kw
                        block = jnp.where(group4 == hq - kh + 1, wide[tap * 16 : tap * 16 + 16], block)
                parts.append(block)
    joined = jnp.concatenate(parts, axis=0)
    w2t[...] = joined.astype(BF)
    w2[...] = joined.T.astype(BF)

    bias_one = column(b1b[...], 16)
    bias_two = column(b2b[...], 32)
    take = iota((256, 512), 1)
    sample = (iota((256, 512), 0) == 2 * (take % 128) - 1 + take // 128).astype(F32).astype(BF)

    def split_columns(part):
        source = raw[:, part * RIM : part * RIM + 64, :].reshape(256, 256)
        columns = dot(source, sample).reshape(4, 64, 512)[:, 8:56]
        for s in range(4):
            shifted[s * 4 : s * 4 + 4, part * RIM : part * RIM + RIM] = columns[
                :, :, s * 128 : (s + 1) * 128
            ].astype(BF)

    lane64 = iota((64, 128), 1)

    def window(p):
        return shifted[:, p * 16 : p * 16 + 32, :].reshape(512, LANES)

    def layer_one(pair):
        both = dot(w1[...], jnp.concatenate([window(p) for p in pair], axis=1))
        for n, p in enumerate(pair):
            linear = both[:, n * 128 : (n + 1) * 128].reshape(32, 16, LANES) + bias_one[None]
            linear = linear.reshape(8, 64, LANES)
            slope = jnp.where(linear > 0, 1.0, 0.3)
            if 2 <= p <= 5:
                slopes[p - 2] = slope
            mean = jnp.sum(linear * slope, axis=0) * 0.125
            if p < 2:
                mean = jnp.where(first, 0.0, mean)
            if p > 5:
                mean = jnp.where(last, 0.0, mean)
            base = p * 192
            pooled[base : base + 64, :] = jnp.where(
                lane64 == 0, 0.0, pltpu.roll(mean, 1, axis=1)
            ).astype(BF)
            pooled[base + 64 : base + 128, :] = mean.astype(BF)
            pooled[base + 128 : base + 192, :] = jnp.where(
                lane64 == 127, 0.0, pltpu.roll(mean, 127, axis=1)
            ).astype(BF)

    def layer_two(pair):
        both = dot(
            w2[...],
            jnp.concatenate([pooled[j * 192 : j * 192 + 576, :] for j in pair], axis=1),
        )
        for n, j in enumerate(pair):
            linear = both[:, n * 128 : (n + 1) * 128].reshape(4, 32, LANES)
            linear = (linear + bias_two[None]).reshape(128, LANES)
            slope = jnp.where(linear > 0, 1.0, 0.3)
            errors_two[j * 128 : (j + 1) * 128, :] = (
                cots[j * 128 : (j + 1) * 128, :].astype(F32) * slope
            ).astype(BF)
            if 1 <= j <= 4:
                out = linear * slope
                for hq in range(4):
                    cotf[pl.ds((j - 1) * 4 + hq, 32, stride=16), :] = out[hq * 32 : (hq + 1) * 32]

    split_columns(1)
    layer_one((3, 4))

    @pl.when(jnp.logical_not(first))
    def _():
        halo(0).wait_recv()

    split_columns(0)

    @pl.when(jnp.logical_not(last))
    def _():
        halo(1).wait_recv()

    split_columns(2)
    layer_one((2, 5))
    layer_one((1, 6))
    layer_one((0, 7))
    layer_two((2, 3))
    layer_two((1, 4))

    @pl.when(jnp.logical_not(first))
    def _():
        halo(2).wait_recv()

    @pl.when(jnp.logical_not(last))
    def _():
        halo(3).wait_recv()

    layer_two((0, 5))
    act_here[...] = cotf[...].astype(BF).reshape(32, 16, LANES)
    act_store = pltpu.make_async_copy(act_here, act_out, out_sem.at[0])
    act_store.start()

    own = jnp.concatenate(
        [errors_two[j * 128 : (j + 1) * 128, :] for j in range(1, 5)], axis=1
    )
    near_in = jnp.concatenate(
        [pooled[j * 192 : j * 192 + 576, :] for j in range(1, 5)], axis=1
    )
    near_in = jnp.concatenate([near_in, jnp.ones((16, 512), BF)], axis=0)
    outer = dot_nt(near_in, own)
    taps = []
    for kd in range(3):
        for kh in range(3):
            for kw in range(3):
                block = jnp.zeros((16, 128), F32)
                for hq in range(4):
                    if 0 <= hq - kh + 1 < 4:
                        at = ((kd * 3 + kw) * 4 + hq) * 16
                        block = jnp.where(group4 == hq - kh + 1, outer[at : at + 16], block)
                taps.append(fold(block, (64, 32)))
    taps.append(fold(outer[576:592], (64, 32)))
    for q in range(7):
        block = taps[4 * q]
        for slot in range(1, 4):
            block = jnp.where(group4 == slot, taps[4 * q + slot], block)
        terms[2 * q] = block[0:8]
        terms[2 * q + 1] = block[8:16]

    terms[14] = jnp.zeros((8, 128), F32)
    terms[15] = jnp.zeros((8, 128), F32)

    share = TILES // space_n

    def scatter(k):
        to = lax.rem(me + k, space_n)
        return pltpu.make_async_remote_copy(
            src_ref=terms.at[pl.ds(to * share, share)],
            dst_ref=landed.at[k - 1],
            send_sem=rs_send.at[k - 1],
            recv_sem=rs_recv.at[k - 1],
            device_id={"space": to},
            device_id_type=MESH,
        )

    def swap(axis, count, k, source, buffer, send, recv):
        return pltpu.make_async_remote_copy(
            src_ref=buffer.at[source],
            dst_ref=buffer.at[source],
            send_sem=send.at[k - 1],
            recv_sem=recv.at[k - 1],
            device_id={axis: lax.rem(lax.axis_index(axis) + k, count)},
            device_id_type=MESH,
        )

    def swap_start(axis, count, *where):
        for k in range(1, count):
            swap(axis, count, k, lax.axis_index(axis), *where).start()

    def swap_sent(axis, count, *where):
        for k in range(1, count):
            swap(axis, count, k, lax.axis_index(axis), *where).wait_send()

    def swap_landed(axis, count, *where):
        for k in range(1, count):
            source = lax.rem(lax.axis_index(axis) + count - k, count)
            swap(axis, count, k, source, *where).wait_recv()

    early_dp = ("dp", dp_n, across, dp_send, dp_recv)
    early_all = ("space", space_n, total, ag_send, ag_recv)
    last_space = ("space", space_n, late_space, ls_send, ls_recv)
    last_dp = ("dp", dp_n, late_dp, ld_send, ld_recv)

    for k in range(1, space_n):
        scatter(k).start()

    back = jnp.concatenate([w2t[kd * 192 : (kd + 1) * 192, :] for kd in (2, 1, 0)], axis=1)
    quad = dot(
        back,
        jnp.concatenate([errors_two[q * 128 : q * 128 + 384, :] for q in range(4)], axis=1),
    )
    for q in range(4):
        three = quad[:, q * 128 : (q + 1) * 128]
        grad = three[64:128]
        grad = grad + jnp.where(lane64 == 127, 0.0, pltpu.roll(three[0:64], 127, axis=1))
        grad = grad + jnp.where(lane64 == 0, 0.0, pltpu.roll(three[128:192], 1, axis=1))
        grad = grad.astype(BF).astype(F32)
        for hq in range(4):
            pgf[pl.ds(q * 4 + hq, 16, stride=16), :] = grad[hq * 16 : (hq + 1) * 16]
        errors_one[:, q * 128 : (q + 1) * 128] = (
            ((grad * 0.125)[None] * slopes[q]).astype(BF).reshape(512, LANES)
        )
    pg_here[...] = pgf[...].astype(BF).reshape(16, 16, LANES)
    pg_store = pltpu.make_async_copy(pg_here, pg_out, out_sem.at[1])
    pg_store.start()

    near_in = jnp.concatenate([window(p) for p in range(2, 6)], axis=1)
    near_in = jnp.concatenate([near_in, jnp.ones((16, 512), BF)], axis=0)
    outer = dot_nt(near_in, errors_one[...])
    body = outer[0:512].reshape(4, 4, 4, 8, 512)
    low = iota((4, 3, 8, 128), 3) < 64
    for kh in range(3):
        summed = jnp.zeros((4, 4, 3, 8, 128), F32)
        for part in range(4):
            dd = part // 2
            cut = body[:, :, dd : dd + 3, :, part * 128 : (part + 1) * 128]
            mask = near[kh][:, part * 128 : (part + 1) * 128]
            summed = summed + jnp.where(mask[None, None, None], cut, 0.0)
        for kw in range(3):
            both = jnp.where(low, summed[kw], summed[kw + 1])
            for kd in range(3):
                tap = (kd * 3 + kh) * 3 + kw
                stack[tap * 32 : tap * 32 + 32, :] = both[:, kd].reshape(32, LANES)
    ones = outer[512:520]
    ones = ones[:, 0:128] + ones[:, 128:256] + ones[:, 256:384] + ones[:, 384:512]
    stack[864:872, :] = jnp.where(iota((8, 128), 0) == 0, ones, 0.0)
    stack[872:896, :] = jnp.zeros((24, 128), F32)
    sums = terms[pl.ds(me * share, share)]
    for k in range(1, space_n):
        scatter(k).wait_recv()
        sums = sums + landed[k - 1]
    across[mine] = sums
    swap_start(*early_dp)

    gather = (iota((112, 896), 0) == iota((112, 896), 1) // 8).astype(F32).astype(BF)
    whole = stack[...]
    high = whole.astype(BF)
    rest = (whole - high.astype(F32)).astype(BF)
    reduced = fold(dot(gather, high) + dot(gather, rest), (64, 32, 16))
    group8 = iota((8, 128), 1) // 16
    for half in range(2):
        block = jnp.zeros((8, 128), F32)
        for slot in range(8):
            v = half * 8 + slot
            if v < 14:
                block = jnp.where(group8 == slot, reduced[v * 8 : v * 8 + 8], block)
        late[half] = block

    late_dp[mine] = late[...]
    swap_start(*last_dp)

    swap_landed(*early_dp)
    sums = across[0]
    for k in range(1, dp_n):
        sums = sums + across[k]
    total[me] = sums
    swap_start(*early_all)

    swap_landed(*last_dp)
    sums = late_dp[0]
    for k in range(1, dp_n):
        sums = sums + late_dp[k]
    late_space[me] = sums
    swap_start(*last_space)

    swap_landed(*early_all)
    sums_here[0:TILES] = total[...].reshape(TILES, 8, 128)
    swap_landed(*last_space)
    sums = late_space[0]
    for k in range(1, space_n):
        sums = sums + late_space[k]
    sums_here[TILES : TILES + 2] = sums
    sums_store = pltpu.make_async_copy(sums_here, sums_out, out_sem.at[2])
    sums_store.start()

    for k in range(1, space_n):
        scatter(k).wait_send()
    swap_sent(*early_dp)
    swap_sent(*early_all)
    swap_sent(*last_space)
    swap_sent(*last_dp)
    act_store.wait()
    pg_store.wait()
    sums_store.wait()

    @pl.when(jnp.logical_not(last))
    def _():
        halo(0).wait_send()
        halo(2).wait_send()

    @pl.when(jnp.logical_not(first))
    def _():
        halo(1).wait_send()
        halo(3).wait_send()


def finish(scale_one, scale_two, act, pg, sums_in, act_out, pg_out, g1_out, s1_out, g2_out, s2_out,
           act_here, pg_here, sums_here, g1, s1, g2, s2, sem):
    load = pltpu.make_async_copy(sums_in, sums_here, sem.at[6])
    load.start()
    loads = [
        pltpu.make_async_copy(act, act_here, sem.at[7]),
        pltpu.make_async_copy(pg, pg_here, sem.at[8]),
    ]
    for copy in loads:
        copy.start()
    big = [
        pltpu.make_async_copy(act_here, act_out, sem.at[0]),
        pltpu.make_async_copy(pg_here, pg_out, sem.at[1]),
    ]
    for ready, copy in zip(loads, big):
        ready.wait()
        copy.start()
    load.wait()
    sums = sums_here[...]
    for q in range(7):
        block = jnp.concatenate([sums[2 * q], sums[2 * q + 1]], axis=0) * scale_two
        for slot in range(4):
            tap = 4 * q + slot
            turned = block if slot == 0 else pltpu.roll(block, 128 - 32 * slot, axis=1)
            if tap < 27:
                g2[tap * 16 : tap * 16 + 16, :] = turned[:, 0:32]
            else:
                s2[...] = turned[0:1, 0:32]
    for v in range(14):
        block = sums[TILES + v // 8] * scale_one
        slot = v % 8
        turned = block if slot == 0 else pltpu.roll(block, 128 - 16 * slot, axis=1)
        g1[2 * v] = turned[0:4, 0:16]
        if v < 13:
            g1[2 * v + 1] = turned[4:8, 0:16]
        else:
            s1[...] = turned[4:5, 0:16]
    small = [
        pltpu.make_async_copy(src, dst, sem.at[2 + n])
        for n, (src, dst) in enumerate(((g1, g1_out), (s1, s1_out), (g2, g2_out), (s2, s2_out)))
    ]
    for copy in small:
        copy.start()
    for copy in big + small:
        copy.wait()


def shards(dp_n, space_n, volume, first_filters, first_biases, second_filters, second_biases, cotangent):
    _, c_in, planes, high, wide = volume.shape
    c1, c2 = first_filters.shape[0], second_filters.shape[0]
    assert (c_in, planes, high, wide, c1, c2) == (4, 8, 8, 256, 16, 32)
    assert TILES % space_n == 0
    count_one = dp_n * space_n * planes * high * wide
    scale_one = 1.0 / math.sqrt(count_one)
    scale_two = 1.0 / math.sqrt(count_one / 8)
    share = TILES // space_n
    f1 = first_filters.transpose(2, 3, 4, 1, 0).reshape(27, 4, 16)
    f2 = second_filters.transpose(2, 3, 4, 1, 0).reshape(432, 32)
    vmem = pl.BlockSpec(memory_space=pltpu.VMEM)
    hbm = pl.BlockSpec(memory_space=pltpu.HBM)
    dma = pltpu.SemaphoreType.DMA
    act, pg, sums = pl.pallas_call(
        functools.partial(kernel, dp_n, space_n),
        out_shape=(
            jax.ShapeDtypeStruct((32, 16, 128), BF),
            jax.ShapeDtypeStruct((16, 16, 128), BF),
            jax.ShapeDtypeStruct((TILES + 2, 8, 128), F32),
        ),
        in_specs=[hbm] * 7,
        out_specs=(hbm,) * 3,
        scratch_shapes=[
            pltpu.VMEM((4, 2 * RIM + 64, 256), BF),
            pltpu.VMEM((32, 16, 128), BF),
            pltpu.VMEM((27, 4, 16), BF),
            pltpu.VMEM((128, 128), F32),
            pltpu.VMEM((432, 32), BF),
            pltpu.VMEM((1, 16), F32),
            pltpu.VMEM((1, 32), F32),
            pltpu.VMEM((768, 128), BF),
            pltpu.VMEM((768, 128), BF),
            pltpu.VMEM((512, 128), F32),
            pltpu.VMEM((16, 144, 128), BF),
            pltpu.VMEM((8 * 192, 128), BF),
            pltpu.VMEM((4, 8, 64, 128), F32),
            pltpu.VMEM((768, 128), BF),
            pltpu.VMEM((512, 512), BF),
            pltpu.VMEM((256, 128), F32),
            pltpu.VMEM((512, 512), BF),
            pltpu.VMEM((128, 576), BF),
            pltpu.VMEM((576, 128), BF),
            pltpu.VMEM((896, 128), F32),
            pltpu.VMEM((TILES, 8, 128), F32),
            pltpu.VMEM((space_n - 1, share, 8, 128), F32),
            pltpu.VMEM((dp_n, share, 8, 128), F32),
            pltpu.VMEM((space_n, share, 8, 128), F32),
            pltpu.VMEM((2, 8, 128), F32),
            pltpu.VMEM((space_n, 2, 8, 128), F32),
            pltpu.VMEM((dp_n, 2, 8, 128), F32),
            pltpu.VMEM((32, 16, 128), BF),
            pltpu.VMEM((16, 16, 128), BF),
            pltpu.VMEM((TILES + 2, 8, 128), F32),
            dma((3,)),
            dma((7,)),
            dma((4,)),
            dma((4,)),
        ]
        + [dma((space_n - 1,))] * 2
        + [dma((dp_n - 1,))] * 2
        + [dma((space_n - 1,))] * 4
        + [dma((dp_n - 1,))] * 2,
        compiler_params=pltpu.CompilerParams(
            collective_id=0, has_side_effects=True, vmem_limit_bytes=VMEM_LIMIT
        ),
    )(
        volume.reshape(4, 64, 256),
        cotangent.reshape(32, 16, 128),
        f1,
        f2,
        first_biases.reshape(1, 16),
        second_biases.reshape(1, 32),
        jnp.asarray(tap_choice(), BF),
    )
    act, pg, g1, s1, g2, s2 = pl.pallas_call(
        functools.partial(finish, scale_one, scale_two),
        out_shape=(
            jax.ShapeDtypeStruct((32, 16, 128), BF),
            jax.ShapeDtypeStruct((16, 16, 128), BF),
            jax.ShapeDtypeStruct((27, 4, 16), F32),
            jax.ShapeDtypeStruct((1, 16), F32),
            jax.ShapeDtypeStruct((432, 32), F32),
            jax.ShapeDtypeStruct((1, 32), F32),
        ),
        in_specs=[hbm] * 3,
        out_specs=(hbm,) * 6,
        scratch_shapes=[
            pltpu.VMEM((32, 16, 128), BF),
            pltpu.VMEM((16, 16, 128), BF),
            pltpu.VMEM((TILES + 2, 8, 128), F32),
            pltpu.VMEM((27, 4, 16), F32),
            pltpu.VMEM((1, 16), F32),
            pltpu.VMEM((432, 32), F32),
            pltpu.VMEM((1, 32), F32),
            dma((9,)),
        ],
        compiler_params=pltpu.CompilerParams(vmem_limit_bytes=VMEM_LIMIT),
    )(act, pg, sums)
    return (
        act.reshape(1, 32, 4, 4, 128),
        pg.reshape(1, 16, 4, 4, 128),
        g1.reshape(3, 3, 3, 4, 16).transpose(4, 3, 0, 1, 2),
        s1.reshape(16),
        g2.reshape(3, 3, 3, 16, 32).transpose(4, 3, 0, 1, 2),
        s2.reshape(32),
    )


def solution(mesh):
    placed = (
        P("dp", None, "space", None, None),
        P(),
        P(),
        P(),
        P(),
        P("dp", None, "space", None, None),
    )
    return jax.shard_map(
        functools.partial(shards, mesh.shape["dp"], mesh.shape["space"]),
        mesh=mesh,
        in_specs=placed,
        out_specs=(
            P("dp", None, "space", None, None),
            P("dp", None, "space", None, None),
            P(),
            P(),
            P(),
            P(),
        ),
        check_vma=False,
    )
```

```python
import functools
import math

import jax
import jax.numpy as jnp
import numpy as np
from jax import lax
from jax.experimental import pallas as pl
from jax.experimental.pallas import tpu as pltpu
from jax.sharding import PartitionSpec as P

BF = jnp.bfloat16
F32 = jnp.float32
MESH = pl.DeviceIdType.MESH
LANES = 128
RIM = 48
VMEM_LIMIT = 60 * 1024 * 1024
TILES = 16


def tap_choice():
    table = np.zeros((2, 2, 3, 4, 4, 4, 128), np.float32)
    for dd in range(2):
        for wpar in range(2):
            for kh in range(3):
                for s in range(4):
                    for dz in range(4):
                        kd, kw = dz - dd, s - wpar
                        if 0 <= kd < 3 and 0 <= kw < 3:
                            for i in range(4):
                                table[dd, wpar, kh, s, i, dz, ((kd * 3 + kh) * 3 + kw) * 4 + i] = 1
    return table.reshape(4 * 192, 128)


def iota(shape, dim):
    return lax.broadcasted_iota(jnp.int32, shape, dim)


def dot(a, b):
    return jnp.dot(a, b, preferred_element_type=F32)


def dot_nt(a, b):
    return lax.dot_general(a, b, (((1,), (1,)), ((), ())), preferred_element_type=F32)


def column(row, count):
    return jnp.sum(
        jnp.where(iota((count, count), 0) == iota((count, count), 1), row, 0.0),
        axis=1,
        keepdims=True,
    )


def fold(values, steps):
    for step in steps:
        values = values + pltpu.roll(values, step, axis=values.ndim - 1)
    return values


def kernel(
    dp_n, space_n,
    vol, cot, f1, f2, b1, b2, choice,
    act_out, pg_out, sums_out,
    raw, cotb, f1b, f1f, f2b, b1b, b2b, chosen,
    cots, cotf, shifted, pooled, slopes, errors_two, errors_one, pgf, w1, w2, w2t,
    stack, terms, landed, across, total, late, late_space, late_dp,
    act_here, pg_here, sums_here, out_sem, in_sem, halo_send, halo_recv, rs_send, rs_recv, dp_send, dp_recv, ag_send, ag_recv,
    ls_send, ls_recv, ld_send, ld_recv,
):
    me = lax.axis_index("space")
    mine = lax.axis_index("dp")
    first = me == 0
    last = me == space_n - 1

    barrier = pltpu.get_barrier_semaphore()
    for k in range(1, space_n):
        pl.semaphore_signal(
            barrier, inc=1, device_id={"space": lax.rem(me + k, space_n)}, device_id_type=MESH
        )
    for k in range(1, dp_n):
        pl.semaphore_signal(
            barrier, inc=1, device_id={"dp": lax.rem(mine + k, dp_n)}, device_id_type=MESH
        )
    loads = [
        pltpu.make_async_copy(src, dst, in_sem.at[n])
        for n, (src, dst) in enumerate(
            (
                (cot, cotb),
                (f1, f1b),
                (choice, chosen),
                (f2, f2b),
                (b1, b1b),
                (b2, b2b),
                (vol, raw.at[:, RIM : RIM + 64]),
            )
        )
    ]
    for load in loads:
        load.start()

    @pl.when(first)
    def _():
        raw[:, 0:RIM, :] = jnp.zeros((4, RIM, 256), BF)
        cots[0:128, :] = jnp.zeros((128, LANES), BF)

    @pl.when(last)
    def _():
        raw[:, RIM + 64 :, :] = jnp.zeros((4, RIM, 256), BF)
        cots[640:768, :] = jnp.zeros((128, LANES), BF)

    right = lax.rem(me + 1, space_n)
    left = lax.rem(me + space_n - 1, space_n)

    def halo(which):
        src, dst, to = (
            (vol.at[:, 16:64], raw.at[:, 0:RIM], right),
            (vol.at[:, 0:RIM], raw.at[:, RIM + 64 : 2 * RIM + 64], left),
            (cots.at[512:640], cots.at[0:128], right),
            (cots.at[128:256], cots.at[640:768], left),
        )[which]
        return pltpu.make_async_remote_copy(
            src_ref=src,
            dst_ref=dst,
            send_sem=halo_send.at[which],
            recv_sem=halo_recv.at[which],
            device_id={"space": to},
            device_id_type=MESH,
        )

    pl.semaphore_wait(barrier, space_n - 1 + dp_n - 1)

    @pl.when(jnp.logical_not(last))
    def _():
        halo(0).start()

    @pl.when(jnp.logical_not(first))
    def _():
        halo(1).start()

    loads[0].wait()
    cotf[...] = cotb[...].reshape(512, LANES).astype(F32)
    for d in range(4):
        for hq in range(4):
            cots[pl.ds((1 + d) * 128 + hq * 32, 32), :] = cotf[
                pl.ds(d * 4 + hq, 32, stride=16), :
            ].astype(BF)

    @pl.when(jnp.logical_not(last))
    def _():
        halo(2).start()

    @pl.when(jnp.logical_not(first))
    def _():
        halo(3).start()

    for load in loads[1:]:
        load.wait()
    f1f[...] = jnp.zeros((128, 128), F32)
    for tap in range(27):
        f1f[tap * 4 : tap * 4 + 4, 0:16] = f1b[tap].astype(F32)

    picked = dot_nt(f1f[...].T[0:16].astype(BF), chosen[...])
    picked = jnp.concatenate([picked[:, g * 64 : (g + 1) * 64] for g in range(12)], axis=0)
    repeat = (iota((64, 512), 0) == iota((64, 512), 1) // 8).astype(F32).astype(BF)
    rows = dot(picked.astype(BF), repeat)
    height = iota((16, 512), 1) % 8
    for dd in range(2):
        for hpar in range(2):
            for wpar in range(2):
                for hq in range(4):
                    block = jnp.zeros((16, 512), F32)
                    for kh in range(3):
                        at = ((dd * 2 + wpar) * 3 + kh) * 16
                        block = jnp.where(
                            height == 2 * hq + hpar + kh - 1, rows[at : at + 16], block
                        )
                    at = (((dd * 2 + hpar) * 2 + wpar) * 4 + hq) * 16
                    w1[at : at + 16, :] = block.astype(BF)
    lane8 = iota((8, 512), 1)
    reach = iota((8, 512), 0) - (2 * ((lane8 // 16) % 4) + (lane8 // 128) % 2) + 1
    near = [reach == kh for kh in range(3)]
    tile4 = (iota((32, 128), 0) == iota((32, 128), 1) % 32).astype(F32).astype(BF)
    wide = dot(f2b[...], tile4)
    group4 = iota((16, 128), 1) // 32
    parts = []
    for kd in range(3):
        for kw in range(3):
            for hq in range(4):
                block = jnp.zeros((16, 128), F32)
                for kh in range(3):
                    if 0 <= hq - kh + 1 < 4:
                        tap = (kd * 3 + kh) * 3 + kw
                        block = jnp.where(group4 == hq - kh + 1, wide[tap * 16 : tap * 16 + 16], block)
                parts.append(block)
    joined = jnp.concatenate(parts, axis=0)
    w2t[...] = joined.astype(BF)
    w2[...] = joined.T.astype(BF)

    bias_one = column(b1b[...], 16)
    bias_two = column(b2b[...], 32)
    take = iota((256, 512), 1)
    sample = (iota((256, 512), 0) == 2 * (take % 128) - 1 + take // 128).astype(F32).astype(BF)

    def split_columns(part):
        source = raw[:, part * RIM : part * RIM + 64, :].reshape(256, 256)
        columns = dot(source, sample).reshape(4, 64, 512)[:, 8:56]
        for s in range(4):
            shifted[s * 4 : s * 4 + 4, part * RIM : part * RIM + RIM] = columns[
                :, :, s * 128 : (s + 1) * 128
            ].astype(BF)

    lane64 = iota((64, 128), 1)

    def window(p):
        return shifted[:, p * 16 : p * 16 + 32, :].reshape(512, LANES)

    def layer_one(pair):
        both = dot(w1[...], jnp.concatenate([window(p) for p in pair], axis=1))
        for n, p in enumerate(pair):
            linear = both[:, n * 128 : (n + 1) * 128].reshape(32, 16, LANES) + bias_one[None]
            linear = linear.reshape(8, 64, LANES)
            slope = jnp.where(linear > 0, 1.0, 0.3)
            if 2 <= p <= 5:
                slopes[p - 2] = slope
            mean = jnp.sum(linear * slope, axis=0) * 0.125
            if p < 2:
                mean = jnp.where(first, 0.0, mean)
            if p > 5:
                mean = jnp.where(last, 0.0, mean)
            base = p * 192
            pooled[base : base + 64, :] = jnp.where(
                lane64 == 0, 0.0, pltpu.roll(mean, 1, axis=1)
            ).astype(BF)
            pooled[base + 64 : base + 128, :] = mean.astype(BF)
            pooled[base + 128 : base + 192, :] = jnp.where(
                lane64 == 127, 0.0, pltpu.roll(mean, 127, axis=1)
            ).astype(BF)

    def layer_two(pair):
        both = dot(
            w2[...],
            jnp.concatenate([pooled[j * 192 : j * 192 + 576, :] for j in pair], axis=1),
        )
        for n, j in enumerate(pair):
            linear = both[:, n * 128 : (n + 1) * 128].reshape(4, 32, LANES)
            linear = (linear + bias_two[None]).reshape(128, LANES)
            slope = jnp.where(linear > 0, 1.0, 0.3)
            errors_two[j * 128 : (j + 1) * 128, :] = (
                cots[j * 128 : (j + 1) * 128, :].astype(F32) * slope
            ).astype(BF)
            if 1 <= j <= 4:
                out = linear * slope
                for hq in range(4):
                    cotf[pl.ds((j - 1) * 4 + hq, 32, stride=16), :] = out[hq * 32 : (hq + 1) * 32]

    split_columns(1)
    layer_one((3, 4))

    @pl.when(jnp.logical_not(first))
    def _():
        halo(0).wait_recv()

    split_columns(0)

    @pl.when(jnp.logical_not(last))
    def _():
        halo(1).wait_recv()

    split_columns(2)
    layer_one((2, 5))
    layer_one((1, 6))
    layer_one((0, 7))
    layer_two((2, 3))
    layer_two((1, 4))

    @pl.when(jnp.logical_not(first))
    def _():
        halo(2).wait_recv()

    @pl.when(jnp.logical_not(last))
    def _():
        halo(3).wait_recv()

    layer_two((0, 5))
    act_here[...] = cotf[...].astype(BF).reshape(32, 16, LANES)
    act_store = pltpu.make_async_copy(act_here, act_out, out_sem.at[0])
    act_store.start()

    own = jnp.concatenate(
        [errors_two[j * 128 : (j + 1) * 128, :] for j in range(1, 5)], axis=1
    )
    near_in = jnp.concatenate(
        [pooled[j * 192 : j * 192 + 576, :] for j in range(1, 5)], axis=1
    )
    near_in = jnp.concatenate([near_in, jnp.ones((16, 512), BF)], axis=0)
    outer = dot_nt(near_in, own)
    taps = []
    for kd in range(3):
        for kh in range(3):
            for kw in range(3):
                block = jnp.zeros((16, 128), F32)
                for hq in range(4):
                    if 0 <= hq - kh + 1 < 4:
                        at = ((kd * 3 + kw) * 4 + hq) * 16
                        block = jnp.where(group4 == hq - kh + 1, outer[at : at + 16], block)
                taps.append(fold(block, (64, 32)))
    taps.append(fold(outer[576:592], (64, 32)))
    for q in range(7):
        block = taps[4 * q]
        for slot in range(1, 4):
            block = jnp.where(group4 == slot, taps[4 * q + slot], block)
        terms[2 * q] = block[0:8]
        terms[2 * q + 1] = block[8:16]

    terms[14] = jnp.zeros((8, 128), F32)
    terms[15] = jnp.zeros((8, 128), F32)

    share = TILES // space_n

    def scatter(k):
        to = lax.rem(me + k, space_n)
        return pltpu.make_async_remote_copy(
            src_ref=terms.at[pl.ds(to * share, share)],
            dst_ref=landed.at[k - 1],
            send_sem=rs_send.at[k - 1],
            recv_sem=rs_recv.at[k - 1],
            device_id={"space": to},
            device_id_type=MESH,
        )

    def swap(axis, count, k, source, buffer, send, recv):
        return pltpu.make_async_remote_copy(
            src_ref=buffer.at[source],
            dst_ref=buffer.at[source],
            send_sem=send.at[k - 1],
            recv_sem=recv.at[k - 1],
            device_id={axis: lax.rem(lax.axis_index(axis) + k, count)},
            device_id_type=MESH,
        )

    def swap_start(axis, count, *where):
        for k in range(1, count):
            swap(axis, count, k, lax.axis_index(axis), *where).start()

    def swap_sent(axis, count, *where):
        for k in range(1, count):
            swap(axis, count, k, lax.axis_index(axis), *where).wait_send()

    def swap_landed(axis, count, *where):
        for k in range(1, count):
            source = lax.rem(lax.axis_index(axis) + count - k, count)
            swap(axis, count, k, source, *where).wait_recv()

    early_dp = ("dp", dp_n, across, dp_send, dp_recv)
    early_all = ("space", space_n, total, ag_send, ag_recv)
    last_space = ("space", space_n, late_space, ls_send, ls_recv)
    last_dp = ("dp", dp_n, late_dp, ld_send, ld_recv)

    back = jnp.concatenate([w2t[kd * 192 : (kd + 1) * 192, :] for kd in (2, 1, 0)], axis=1)
    quad = dot(
        back,
        jnp.concatenate([errors_two[q * 128 : q * 128 + 384, :] for q in range(4)], axis=1),
    )
    for q in range(4):
        three = quad[:, q * 128 : (q + 1) * 128]
        grad = three[64:128]
        grad = grad + jnp.where(lane64 == 127, 0.0, pltpu.roll(three[0:64], 127, axis=1))
        grad = grad + jnp.where(lane64 == 0, 0.0, pltpu.roll(three[128:192], 1, axis=1))
        grad = grad.astype(BF).astype(F32)
        for hq in range(4):
            pgf[pl.ds(q * 4 + hq, 16, stride=16), :] = grad[hq * 16 : (hq + 1) * 16]
        errors_one[:, q * 128 : (q + 1) * 128] = (
            ((grad * 0.125)[None] * slopes[q]).astype(BF).reshape(512, LANES)
        )
    pg_here[...] = pgf[...].astype(BF).reshape(16, 16, LANES)
    pg_store = pltpu.make_async_copy(pg_here, pg_out, out_sem.at[1])
    pg_store.start()

    for k in range(1, space_n):
        scatter(k).start()

    near_in = jnp.concatenate([window(p) for p in range(2, 6)], axis=1)
    near_in = jnp.concatenate([near_in, jnp.ones((16, 512), BF)], axis=0)
    outer = dot_nt(near_in, errors_one[...])
    body = outer[0:512].reshape(4, 4, 4, 8, 512)
    low = iota((4, 3, 8, 128), 3) < 64
    for kh in range(3):
        summed = jnp.zeros((4, 4, 3, 8, 128), F32)
        for part in range(4):
            dd = part // 2
            cut = body[:, :, dd : dd + 3, :, part * 128 : (part + 1) * 128]
            mask = near[kh][:, part * 128 : (part + 1) * 128]
            summed = summed + jnp.where(mask[None, None, None], cut, 0.0)
        for kw in range(3):
            both = jnp.where(low, summed[kw], summed[kw + 1])
            for kd in range(3):
                tap = (kd * 3 + kh) * 3 + kw
                stack[tap * 32 : tap * 32 + 32, :] = both[:, kd].reshape(32, LANES)
    ones = outer[512:520]
    ones = ones[:, 0:128] + ones[:, 128:256] + ones[:, 256:384] + ones[:, 384:512]
    stack[864:872, :] = jnp.where(iota((8, 128), 0) == 0, ones, 0.0)
    stack[872:896, :] = jnp.zeros((24, 128), F32)
    gather = (iota((112, 896), 0) == iota((112, 896), 1) // 8).astype(F32).astype(BF)
    whole = stack[...]
    high = whole.astype(BF)
    rest = (whole - high.astype(F32)).astype(BF)
    reduced = fold(dot(gather, high) + dot(gather, rest), (64, 32, 16))
    group8 = iota((8, 128), 1) // 16
    for half in range(2):
        block = jnp.zeros((8, 128), F32)
        for slot in range(8):
            v = half * 8 + slot
            if v < 14:
                block = jnp.where(group8 == slot, reduced[v * 8 : v * 8 + 8], block)
        late[half] = block

    late_space[me] = late[...]
    swap_start(*last_space)

    sums = terms[pl.ds(me * share, share)]
    for k in range(1, space_n):
        scatter(k).wait_recv()
        sums = sums + landed[k - 1]
    across[mine] = sums
    swap_start(*early_dp)

    swap_landed(*last_space)
    sums = late_space[0]
    for k in range(1, space_n):
        sums = sums + late_space[k]
    late_dp[mine] = sums
    swap_start(*last_dp)

    swap_landed(*early_dp)
    sums = across[0]
    for k in range(1, dp_n):
        sums = sums + across[k]
    total[me] = sums
    swap_start(*early_all)

    swap_landed(*early_all)
    sums_here[0:TILES] = total[...].reshape(TILES, 8, 128)
    swap_landed(*last_dp)
    sums = late_dp[0]
    for k in range(1, dp_n):
        sums = sums + late_dp[k]
    sums_here[TILES : TILES + 2] = sums
    sums_store = pltpu.make_async_copy(sums_here, sums_out, out_sem.at[2])
    sums_store.start()

    for k in range(1, space_n):
        scatter(k).wait_send()
    swap_sent(*early_dp)
    swap_sent(*early_all)
    swap_sent(*last_space)
    swap_sent(*last_dp)
    act_store.wait()
    pg_store.wait()
    sums_store.wait()

    @pl.when(jnp.logical_not(last))
    def _():
        halo(0).wait_send()
        halo(2).wait_send()

    @pl.when(jnp.logical_not(first))
    def _():
        halo(1).wait_send()
        halo(3).wait_send()


def finish(scale_one, scale_two, act, pg, sums_in, act_out, pg_out, g1_out, s1_out, g2_out, s2_out,
           act_here, pg_here, sums_here, g1, s1, g2, s2, sem):
    load = pltpu.make_async_copy(sums_in, sums_here, sem.at[6])
    load.start()
    loads = [
        pltpu.make_async_copy(act, act_here, sem.at[7]),
        pltpu.make_async_copy(pg, pg_here, sem.at[8]),
    ]
    for copy in loads:
        copy.start()
    big = [
        pltpu.make_async_copy(act_here, act_out, sem.at[0]),
        pltpu.make_async_copy(pg_here, pg_out, sem.at[1]),
    ]
    for ready, copy in zip(loads, big):
        ready.wait()
        copy.start()
    load.wait()
    sums = sums_here[...]
    for q in range(7):
        block = jnp.concatenate([sums[2 * q], sums[2 * q + 1]], axis=0) * scale_two
        for slot in range(4):
            tap = 4 * q + slot
            turned = block if slot == 0 else pltpu.roll(block, 128 - 32 * slot, axis=1)
            if tap < 27:
                g2[tap * 16 : tap * 16 + 16, :] = turned[:, 0:32]
            else:
                s2[...] = turned[0:1, 0:32]
    for v in range(14):
        block = sums[TILES + v // 8] * scale_one
        slot = v % 8
        turned = block if slot == 0 else pltpu.roll(block, 128 - 16 * slot, axis=1)
        g1[2 * v] = turned[0:4, 0:16]
        if v < 13:
            g1[2 * v + 1] = turned[4:8, 0:16]
        else:
            s1[...] = turned[4:5, 0:16]
    small = [
        pltpu.make_async_copy(src, dst, sem.at[2 + n])
        for n, (src, dst) in enumerate(((g1, g1_out), (s1, s1_out), (g2, g2_out), (s2, s2_out)))
    ]
    for copy in small:
        copy.start()
    for copy in big + small:
        copy.wait()


def shards(dp_n, space_n, volume, first_filters, first_biases, second_filters, second_biases, cotangent):
    _, c_in, planes, high, wide = volume.shape
    c1, c2 = first_filters.shape[0], second_filters.shape[0]
    assert (c_in, planes, high, wide, c1, c2) == (4, 8, 8, 256, 16, 32)
    assert TILES % space_n == 0
    count_one = dp_n * space_n * planes * high * wide
    scale_one = 1.0 / math.sqrt(count_one)
    scale_two = 1.0 / math.sqrt(count_one / 8)
    share = TILES // space_n
    f1 = first_filters.transpose(2, 3, 4, 1, 0).reshape(27, 4, 16)
    f2 = second_filters.transpose(2, 3, 4, 1, 0).reshape(432, 32)
    vmem = pl.BlockSpec(memory_space=pltpu.VMEM)
    hbm = pl.BlockSpec(memory_space=pltpu.HBM)
    dma = pltpu.SemaphoreType.DMA
    act, pg, sums = pl.pallas_call(
        functools.partial(kernel, dp_n, space_n),
        out_shape=(
            jax.ShapeDtypeStruct((32, 16, 128), BF),
            jax.ShapeDtypeStruct((16, 16, 128), BF),
            jax.ShapeDtypeStruct((TILES + 2, 8, 128), F32),
        ),
        in_specs=[hbm] * 7,
        out_specs=(hbm,) * 3,
        scratch_shapes=[
            pltpu.VMEM((4, 2 * RIM + 64, 256), BF),
            pltpu.VMEM((32, 16, 128), BF),
            pltpu.VMEM((27, 4, 16), BF),
            pltpu.VMEM((128, 128), F32),
            pltpu.VMEM((432, 32), BF),
            pltpu.VMEM((1, 16), F32),
            pltpu.VMEM((1, 32), F32),
            pltpu.VMEM((768, 128), BF),
            pltpu.VMEM((768, 128), BF),
            pltpu.VMEM((512, 128), F32),
            pltpu.VMEM((16, 144, 128), BF),
            pltpu.VMEM((8 * 192, 128), BF),
            pltpu.VMEM((4, 8, 64, 128), F32),
            pltpu.VMEM((768, 128), BF),
            pltpu.VMEM((512, 512), BF),
            pltpu.VMEM((256, 128), F32),
            pltpu.VMEM((512, 512), BF),
            pltpu.VMEM((128, 576), BF),
            pltpu.VMEM((576, 128), BF),
            pltpu.VMEM((896, 128), F32),
            pltpu.VMEM((TILES, 8, 128), F32),
            pltpu.VMEM((space_n - 1, share, 8, 128), F32),
            pltpu.VMEM((dp_n, share, 8, 128), F32),
            pltpu.VMEM((space_n, share, 8, 128), F32),
            pltpu.VMEM((2, 8, 128), F32),
            pltpu.VMEM((space_n, 2, 8, 128), F32),
            pltpu.VMEM((dp_n, 2, 8, 128), F32),
            pltpu.VMEM((32, 16, 128), BF),
            pltpu.VMEM((16, 16, 128), BF),
            pltpu.VMEM((TILES + 2, 8, 128), F32),
            dma((3,)),
            dma((7,)),
            dma((4,)),
            dma((4,)),
        ]
        + [dma((space_n - 1,))] * 2
        + [dma((dp_n - 1,))] * 2
        + [dma((space_n - 1,))] * 4
        + [dma((dp_n - 1,))] * 2,
        compiler_params=pltpu.CompilerParams(
            collective_id=0, has_side_effects=True, vmem_limit_bytes=VMEM_LIMIT
        ),
    )(
        volume.reshape(4, 64, 256),
        cotangent.reshape(32, 16, 128),
        f1,
        f2,
        first_biases.reshape(1, 16),
        second_biases.reshape(1, 32),
        jnp.asarray(tap_choice(), BF),
    )
    act, pg, g1, s1, g2, s2 = pl.pallas_call(
        functools.partial(finish, scale_one, scale_two),
        out_shape=(
            jax.ShapeDtypeStruct((32, 16, 128), BF),
            jax.ShapeDtypeStruct((16, 16, 128), BF),
            jax.ShapeDtypeStruct((27, 4, 16), F32),
            jax.ShapeDtypeStruct((1, 16), F32),
            jax.ShapeDtypeStruct((432, 32), F32),
            jax.ShapeDtypeStruct((1, 32), F32),
        ),
        in_specs=[hbm] * 3,
        out_specs=(hbm,) * 6,
        scratch_shapes=[
            pltpu.VMEM((32, 16, 128), BF),
            pltpu.VMEM((16, 16, 128), BF),
            pltpu.VMEM((TILES + 2, 8, 128), F32),
            pltpu.VMEM((27, 4, 16), F32),
            pltpu.VMEM((1, 16), F32),
            pltpu.VMEM((432, 32), F32),
            pltpu.VMEM((1, 32), F32),
            dma((9,)),
        ],
        compiler_params=pltpu.CompilerParams(vmem_limit_bytes=VMEM_LIMIT),
    )(act, pg, sums)
    return (
        act.reshape(1, 32, 4, 4, 128),
        pg.reshape(1, 16, 4, 4, 128),
        g1.reshape(3, 3, 3, 4, 16).transpose(4, 3, 0, 1, 2),
        s1.reshape(16),
        g2.reshape(3, 3, 3, 16, 32).transpose(4, 3, 0, 1, 2),
        s2.reshape(32),
    )


def solution(mesh):
    placed = (
        P("dp", None, "space", None, None),
        P(),
        P(),
        P(),
        P(),
        P("dp", None, "space", None, None),
    )
    return jax.shard_map(
        functools.partial(shards, mesh.shape["dp"], mesh.shape["space"]),
        mesh=mesh,
        in_specs=placed,
        out_specs=(
            P("dp", None, "space", None, None),
            P("dp", None, "space", None, None),
            P(),
            P(),
            P(),
            P(),
        ),
        check_vma=False,
    )
```
